1024 devices in a mesh: ctx: 32 (over y, z_hi), exp: 8 (over z_lo, core), dp: 4 (over x).
Axes of the slice: x: 4, y: 8, z: 16 (z_hi: 4, z_lo: 4; z = z_hi * 4 + z_lo), core: 2. Of those that a mesh axis runs over, the one named last changes fastest.
Arguments:
- queries: bfloat16 [4, 4096, 4096], P('dp', 'ctx', 'exp'), may hold values from -250 to 250
- key_values: bfloat16 [4, 4096, 1024], P('dp', 'ctx', 'exp'), may hold values from -5 to 5
- out_weight: bfloat16 [4096, 2880], P('exp'), may hold values from -0.09375 to 0.09375
- resid: bfloat16 [4, 4096, 2880], P('dp', ('ctx', 'exp')), may hold values from -45 to 45
- norm_gain: float32 [2880], replicated, may hold values from 0.5 to 1.5
- expert_ids: int32 [4, 4096, 2], P('dp', ('ctx', 'exp')), may hold values from 0 to 7, all different within a row; in each aligned block of 16 rows (0 to 15, 16 to 31, ..., all dimensions but the last counted through in order) at most 8 rows name the same one
- route_weights: float32 [4, 4096, 2], P('dp', ('ctx', 'exp')), may hold values from 0.1 to 1
- w_gate_up: bfloat16 [8, 2, 2880, 1536], P('exp', None, None, 'dp'), may hold values from -0.109375 to 0.109375
- w_down: bfloat16 [8, 1536, 2880], P('exp', 'dp'), may hold values from -0.15625 to 0.15625
Outputs:
- attended: bfloat16 [4, 4096, 2880], P('dp', ('ctx', 'exp'))
- expert_mix: bfloat16 [4, 4096, 2880], P('dp', ('ctx', 'exp'))
The draws below stay inside these ranges and needn't reach their ends.
Inputs may be any that keep to these rules, and one draw needn't show every extreme that they name: `expert_ids`: A token's 2 experts differ. In each aligned block of 16 rows (the tokens of one device) no expert is named by more than 8 rows.
All inputs are finite; a program needn't handle non-finite values.
Results may differ from the reference program's by a relative error of at most 0.02.
Values may be sent and summed in bfloat16 or wider, within the bound.
A program may use at most 32 MiB of HBM per device.

```python
import math
import jax
import jax.numpy as jnp
import numpy as np
from jax import lax

D = 2880
HD = 64
QH_DEV = 8
FF = 1536
TOPK = 2
TOK_DEV = 16
SEQ = 4096
Q_HEADS = 64
KV_HEADS = 8
EXPERTS = 8
CAP = 8
N_DP = 4


def key_rows(key):
    normal_keys = jax.random.normal(key, (N_DP, SEQ, KV_HEADS, HD), jnp.float32)
    return jnp.clip(normal_keys, -5.0, 5.0)


def draw_queries(key, part):
    key = jax.random.fold_in(key, 3)
    array_shape = (N_DP, SEQ, KV_HEADS, QH_DEV, HD)
    drawn = 2.5 * jnp.clip(jax.random.normal(key, array_shape, jnp.float32), -6.0, 6.0)
    return drawn.reshape(N_DP, SEQ, KV_HEADS * QH_DEV * HD).astype(jnp.bfloat16)


def draw_key_values(key, part):
    shared_keys = key_rows(key)
    key = jax.random.fold_in(key, 5)
    array_shape = (N_DP, SEQ, KV_HEADS, HD)
    value_rows = jnp.clip(jax.random.normal(key, array_shape, jnp.float32), -5.0, 5.0)
    return jnp.stack([shared_keys, value_rows], axis=3).reshape(N_DP, SEQ, KV_HEADS * 2 * HD).astype(jnp.bfloat16)


def draw_resid(key, part):
    key = jax.random.fold_in(key, 7)
    row_key, col_key, value_key = jax.random.split(key, 3)
    row_scale = jnp.exp(jax.random.uniform(row_key, (N_DP, SEQ, 1), jnp.float32, math.log(0.3), math.log(3.0)))
    col_scale = jnp.exp(jax.random.uniform(col_key, (1, 1, D), jnp.float32, math.log(0.3), math.log(3.0)))
    values = jnp.clip(jax.random.normal(value_key, (N_DP, SEQ, D), jnp.float32), -5.0, 5.0)
    return (values * row_scale * col_scale).astype(jnp.bfloat16)


def block_scale(key, extent, shards, smallest, top_value):
    loudness, own = 1.0, jax.random.fold_in(key, 6)
    for axis_at, shards_of in shards:
        heights = jnp.exp(jax.random.uniform(jax.random.fold_in(own, axis_at), (shards_of,), jnp.float32, smallest / len(shards), top_value / len(shards)))
        loudness = loudness * jnp.repeat(heights, extent[axis_at] // shards_of).reshape([-1 if axis == axis_at else 1 for axis in range(len(extent))])
    return loudness


def routed_block(key, own, number, rows, count, top, bound, lean):
    order = jax.random.permutation(key, count)
    packed, common = load_shares(count, rows * top, bound, lean, True), load_shares(count, rows * top, bound, lean, False)
    places = jnp.arange(count)

    def named(tallies, rotation):
        used = int((tallies > 0).sum())
        fixed = max(1, used // 4)
        moved = fixed + (places - fixed + rotation * (used - fixed)) % max(1, count - fixed)
        return jnp.zeros((count,), jnp.int32).at[order[jnp.where(places < fixed, places, moved)]].set(jnp.asarray(tallies, jnp.int32))

    tallies = jnp.where(number % 4 == 0, named(packed, number // 4), named(common, number - number // 4 - 1))
    mixed = jax.random.permutation(jax.random.fold_in(own, 3), count)
    donor, taker = mixed[0:count // 2 * 2:2], mixed[1:count // 2 * 2:2]
    slack = jnp.minimum(tallies[donor] - 1, bound - tallies[taker]) // 2
    slack = jnp.where((donor == order[0]) | (taker == order[0]) | (tallies[taker] == 0), 0, jnp.maximum(slack, 0))
    moved = jax.random.randint(jax.random.fold_in(own, 4), (count // 2,), 0, 1 << 20) % (slack + 1)
    tallies = tallies.at[donor].add(-moved).at[taker].add(moved)
    items = jnp.searchsorted(jnp.cumsum(tallies), jnp.arange(rows * top), side="right").astype(jnp.int32)
    listing = items.reshape(top, rows).T
    listing = listing[jax.random.permutation(jax.random.fold_in(own, 1), rows)]
    rotation = jax.random.randint(jax.random.fold_in(own, 2), (rows, 1), 0, top)
    return jnp.take_along_axis(listing, (jnp.arange(top)[None, :] + rotation) % top, axis=1)


def load_shares(count, total, most, lean, full):
    weights = [(1 << 20) // math.isqrt(standing ** lean) + 1 for standing in range(1, count + 1)]
    largest = most if full else min(most, max(-(-total // count), total * weights[0] // sum(weights)))
    least = 1 if total - largest >= count - 1 else 0
    counts, surplus = [largest] + [least] * (count - 1), total - largest - least * (count - 1)
    while surplus > 0:
        free = [i for i in range(1, count) if counts[i] < largest] or [i for i in range(1, count) if counts[i] < most]
        pool, remaining = sum([weights[i] for i in free]), surplus
        for i in free:
            extra = min(most - counts[i], max(1, remaining * weights[i] // pool), surplus)
            counts[i] = counts[i] + extra
            surplus = surplus - extra
    return np.array(counts)


def bell_draw(stream_key, shape, deviation, most, cuts=(), held_as=jnp.bfloat16):
    level = block_scale(stream_key, shape, cuts, -0.22, 0.18) if cuts else 1.0
    entries = jax.random.normal(stream_key, shape, jnp.float32) * deviation * level
    return jnp.minimum(jnp.maximum(entries, -most), most).astype(held_as)


def setup_inputs(seed: int = 0) -> dict:
    key_of = jax.random.split(jax.random.key(seed), 10)
    queries = draw_queries(jax.random.fold_in(key_of[9], 71), 0)
    key_values = draw_key_values(jax.random.fold_in(key_of[9], 71), 0)
    out_weight = bell_draw(key_of[2], (Q_HEADS * HD, D), (Q_HEADS * HD) ** -0.5, 0.09375, ((0, 8),))
    resid = draw_resid(jax.random.fold_in(key_of[9], 71), 0)
    norm_gain = jnp.clip(1.0 + 0.1 * jax.random.normal(key_of[4], (D,), jnp.float32), 0.5, 1.5)
    expert_ids_keys = jax.random.split(jax.random.fold_in(key_of[5], 1), N_DP * SEQ // TOK_DEV)
    expert_ids_turns = jax.random.permutation(jax.random.fold_in(key_of[5], 3), N_DP * SEQ // TOK_DEV)
    expert_ids = jax.vmap(lambda own, number: routed_block(jax.random.fold_in(key_of[5], 2), own, number, TOK_DEV, EXPERTS, TOPK, CAP, 2))(expert_ids_keys, expert_ids_turns).reshape((N_DP, SEQ, TOPK))
    route_weights = jnp.clip(0.1 + 0.9 * jax.random.uniform(key_of[6], (N_DP, SEQ, TOPK), jnp.float32) ** block_scale(key_of[6], (N_DP, SEQ, TOPK), ((0, 4), (1, 256)), -0.2, 0.2), 0.1, 1.0)
    w_gate_up = bell_draw(key_of[7], (EXPERTS, 2, D, FF), D ** -0.5, 0.109375, ((0, 8), (3, 4)))
    w_down = bell_draw(key_of[8], (EXPERTS, FF, D), FF ** -0.5, 0.15625, ((0, 8), (1, 4)))
    return {"queries": queries, "key_values": key_values, "out_weight": out_weight, "resid": resid, "norm_gain": norm_gain, "expert_ids": expert_ids, "route_weights": route_weights, "w_gate_up": w_gate_up, "w_down": w_down}


def expert_rows(rows, expert_idx, w_gate_up, w_down):
    gate_value = jnp.dot(rows, w_gate_up[expert_idx, 0], preferred_element_type=jnp.float32)
    up_value = jnp.dot(rows, w_gate_up[expert_idx, 1], preferred_element_type=jnp.float32)
    activation = (gate_value * jax.nn.sigmoid(1.702 * gate_value) * (up_value + 1.0)).astype(jnp.bfloat16)
    slice_width = FF // N_DP
    running = jnp.zeros((rows.shape[0], D), jnp.float32)
    for slice_idx in range(N_DP):
        lower = slice_idx * slice_width
        part_out = jnp.dot(activation[:, lower:lower + slice_width], w_down[expert_idx, lower:lower + slice_width], preferred_element_type=jnp.float32).astype(jnp.bfloat16)
        running = running + lax.optimization_barrier(part_out).astype(jnp.float32)
    return running

def reference(queries, key_values, out_weight, resid, norm_gain, expert_ids, route_weights, w_gate_up, w_down):
    score_scale = 1.0 / math.sqrt(HD)
    query_heads = queries.reshape(N_DP, SEQ, Q_HEADS, HD).transpose(0, 2, 1, 3).reshape(N_DP * Q_HEADS, SEQ, HD)
    split_kv = key_values.reshape(N_DP, SEQ, KV_HEADS, 2, HD)
    key_heads = split_kv[:, :, :, 0].transpose(0, 2, 1, 3).reshape(N_DP * KV_HEADS, SEQ, HD)
    value_heads = split_kv[:, :, :, 1].transpose(0, 2, 1, 3).reshape(N_DP * KV_HEADS, SEQ, HD)
    position = jnp.arange(SEQ, dtype=jnp.int32)
    visible = position[None, :] <= position[:, None]

    def one_head(head_idx):
        sequence = head_idx // Q_HEADS
        kv_index = sequence * KV_HEADS + head_idx % Q_HEADS // QH_DEV
        scores = jnp.dot(query_heads[head_idx], key_heads[kv_index].T, preferred_element_type=jnp.float32) * score_scale
        row_max = lax.optimization_barrier(jnp.max(jnp.where(visible, scores, -1e+30), axis=-1, keepdims=True))
        probs = jnp.where(visible, jnp.exp(scores - row_max), 0.0)
        summed = jnp.dot(probs.astype(jnp.bfloat16), value_heads[kv_index], preferred_element_type=jnp.float32)
        return (summed / lax.optimization_barrier(jnp.sum(probs, axis=-1, keepdims=True))).astype(jnp.bfloat16)
    head_out = lax.map(one_head, jnp.arange(N_DP * Q_HEADS, dtype=jnp.int32))
    attention = head_out.reshape(N_DP, Q_HEADS, SEQ, HD).transpose(0, 2, 1, 3).reshape(N_DP * SEQ, Q_HEADS * HD)
    projected = jnp.dot(attention, out_weight, preferred_element_type=jnp.float32)
    attended = projected.astype(jnp.bfloat16).reshape(N_DP, SEQ, D)
    hidden_state = resid.reshape(N_DP * SEQ, D).astype(jnp.float32) + projected
    normed = (hidden_state * lax.rsqrt(lax.optimization_barrier(jnp.mean(hidden_state * hidden_state, axis=-1, keepdims=True)) + 1e-05) * norm_gain).astype(jnp.bfloat16)
    block_count = N_DP * SEQ // TOK_DEV
    route_total = TOK_DEV * TOPK
    token_blocks = normed.reshape(block_count, TOK_DEV, D)
    padded = jnp.concatenate([token_blocks, jnp.zeros((block_count, 1, D), jnp.bfloat16)], axis=1)
    chosen_ids = expert_ids.reshape(block_count, route_total)
    matches = (chosen_ids[:, :, None] == jnp.arange(EXPERTS, dtype=jnp.int32)[None, None, :]).astype(jnp.int32)
    slot_index = lax.optimization_barrier(jnp.sum((jnp.cumsum(matches, axis=1) - matches) * matches, axis=-1)).astype(jnp.int32)
    token_of_route = (jnp.arange(route_total, dtype=jnp.int32) // TOPK).astype(jnp.int32)
    weight_rows = route_weights.reshape(block_count, route_total)
    block_index = jnp.arange(block_count, dtype=jnp.int32)[:, None]

    def per_expert(running, expert_idx):
        owned = chosen_ids == expert_idx
        where_slot = jnp.where(owned, slot_index, CAP).astype(jnp.int32)
        table = jnp.full((block_count, CAP), TOK_DEV, jnp.int32).at[block_index, where_slot].set(jnp.broadcast_to(token_of_route[None, :], (block_count, route_total)), mode='drop')
        rows = jax.vmap(lambda block_rows, picks: block_rows[picks])(padded, table)
        outputs = expert_rows(rows.reshape(block_count * CAP, D), expert_idx, w_gate_up, w_down).reshape(block_count, CAP, D)
        spread = (slot_index[:, :, None] == jnp.arange(CAP, dtype=jnp.int32)[None, None, :]) & owned[:, :, None]
        combiner = jnp.where(spread, weight_rows[:, :, None], 0.0).reshape(block_count, TOK_DEV, TOPK, CAP).sum(axis=2)
        running = running + jnp.einsum('bts,bsd->btd', combiner.astype(jnp.float32), outputs, precision=lax.Precision.HIGHEST)
        return (running, None)
    mixture, _ = lax.scan(per_expert, jnp.zeros((block_count, TOK_DEV, D), jnp.float32), jnp.arange(EXPERTS, dtype=jnp.int32))
    expert_mix = mixture.astype(jnp.bfloat16).reshape(N_DP, SEQ, D)
    return (attended, expert_mix)
```

```python
import functools
import math

import jax
import jax.numpy as jnp
from jax import lax
from jax.experimental import pallas as pl
from jax.experimental.pallas import tpu as pltpu
from jax.sharding import PartitionSpec as P

HD = 64
YS = 8
ZH = 4
ZL = 4
XS = 4
MESH = pl.DeviceIdType.MESH
F32 = jnp.float32
BF16 = jnp.bfloat16
SCALE = math.log2(math.e) / math.sqrt(HD)
VMEM_BYTES = 56 * 1024 * 1024


def push(src, dst, send_sem, recv_sem, device):
    return pltpu.make_async_remote_copy(
        src_ref=src,
        dst_ref=dst,
        send_sem=send_sem,
        recv_sem=recv_sem,
        device_id=device,
        device_id_type=MESH,
    )


def column_tiles(width, step):
    return [(start, min(step, width - start)) for start in range(0, width, step)]


def barrier_with(devices):
    barrier = pltpu.get_barrier_semaphore()
    for device in devices:
        pl.semaphore_signal(barrier, inc=1, device_id=device, device_id_type=MESH)
    pl.semaphore_wait(barrier, len(devices))


def attention_kernel(
    q_ref,
    kv_ref,
    w_hbm,
    resid_ref,
    gain_ref,
    ids_ref,
    rw_ref,
    attended_ref,
    payload_ref,
    kv_all,
    qt,
    vt,
    top,
    acc,
    attn,
    w_ref,
    part,
    sib,
    mine,
    landed,
    w_sem,
    kv_sem,
    z_send,
    z_recv,
    f_send,
    f_recv,
    b_send,
    b_recv,
    s_send,
    s_recv,
    r_send,
    r_recv,
):
    ctx = lax.axis_index("ctx")
    y, z = lax.div(ctx, ZH), lax.rem(ctx, ZH)
    exp = lax.axis_index("exp")
    zl, core = lax.div(exp, 2), lax.rem(exp, 2)
    tokens, width = q_ref.shape
    heads = width // HD
    cols = tokens * heads
    model = w_ref.shape[1]
    rows = resid_ref.shape[0]

    up = {"ctx": lax.rem(y + 1, YS) * ZH + z}
    down = {"ctx": lax.rem(y + YS - 1, YS) * ZH + z}
    z_peer = [{"ctx": y * ZH + lax.rem(z + d, ZH)} for d in range(ZH)]
    sibling = {"exp": zl * 2 + 1 - core}
    l_peer = [{"exp": lax.rem(zl + d, ZL) * 2 + core} for d in range(ZL)]

    w_copy = pltpu.make_async_copy(w_hbm, w_ref, w_sem)
    w_copy.start()
    own_copy = pltpu.make_async_copy(kv_ref, kv_all.at[y, z], kv_sem)
    own_copy.start()
    barrier_with([up, down, sibling] + z_peer[1:] + l_peer[1:])

    shift = [0, 1, 3, 2]
    column = [lax.rem(z + ZH - s, ZH) for s in shift]

    def block(group, j):
        return kv_all.at[group, column[j]]

    def forward(group, step, j):
        src = kv_ref if j == 0 and step == 0 else block(group, j)
        return push(src, block(group, j), f_send.at[step, j], f_recv.at[step, j], up)

    def backward(group, step, j):
        src = kv_ref if j == 0 and step == 0 else block(group, j)
        return push(src, block(group, j), b_send.at[step, j], b_recv.at[step, j], down)

    def z_push(j):
        return push(
            kv_ref, kv_all.at[y, z], z_send.at[j - 1], z_recv.at[j - 1], z_peer[shift[j]]
        )

    sends_up = y < YS - 1
    sends_down = y <= 2

    @pl.when(sends_up)
    def _():
        forward(y, 0, 0).start()

    @pl.when(sends_down)
    def _():
        backward(y, 0, 0).start()

    for j in (1, 2, 3):
        z_push(j).start()

    for pair in range(heads // 2):
        turned = q_ref[:, pair * 128 : pair * 128 + 128].astype(F32).T.astype(BF16)
        qt[0:HD, 2 * pair * tokens : (2 * pair + 1) * tokens] = turned[0:HD]
        qt[0:HD, (2 * pair + 1) * tokens : (2 * pair + 2) * tokens] = turned[HD:]
    qt[HD:, :] = jnp.zeros((128 - HD, cols), BF16)
    vt[HD:, :] = jnp.ones((vt.shape[0] - HD, vt.shape[1]), BF16)
    top[...] = jnp.full(top.shape, -1e30, F32)
    acc[...] = jnp.zeros(acc.shape, F32)
    own_copy.wait()

    def attend(group, masked):
        for b in range(ZH):
            turned = kv_all[group, b].astype(F32).T
            vt[0:HD, b * tokens : (b + 1) * tokens] = turned[HD:].astype(BF16)

        def tile(t, carry):
            lanes = pl.ds(pl.multiple_of(t * 256, 256), 256)
            keys = kv_all[group].reshape(ZH * tokens, 2 * HD)
            scores = jnp.dot(keys, qt[:, lanes], preferred_element_type=F32)
            if masked:
                key_pos = lax.broadcasted_iota(jnp.int32, scores.shape, 0)
                query_pos = lax.broadcasted_iota(jnp.int32, scores.shape, 1) % tokens + z * tokens
                scores = jnp.where(key_pos <= query_pos, scores, -1e30)
            old = top[:, lanes]
            new = jnp.maximum(old, jnp.max(scores, axis=0, keepdims=True))
            probs = jnp.exp2((scores - new) * SCALE).astype(BF16)
            decay = jnp.exp2((old - new) * SCALE)
            top[:, lanes] = new
            acc[:, lanes] = acc[:, lanes] * decay + jnp.dot(
                vt[...], probs, preferred_element_type=F32
            )
            return carry

        lax.fori_loop(0, cols // 256, tile, 0)

    for j in (1, 2, 3):
        z_push(j).wait_recv()

        @pl.when(sends_up)
        def _():
            forward(y, 0, j).start()

        @pl.when(sends_down)
        def _():
            backward(y, 0, j).start()

    attend(y, True)

    for step in (1, 2, 3, 4):
        group = y - step

        @pl.when(group >= 0)
        def _():
            for j in range(ZH):
                forward(group, step - 1, j).wait_recv()
                if step < 4:

                    @pl.when(sends_up)
                    def _():
                        forward(group, step, j).start()

            attend(group, False)

        if step < 4:
            wrapped = lax.rem(y + step, YS)

            @pl.when(wrapped <= 2)
            def _():
                for j in range(ZH):
                    backward(wrapped, step - 1, j).wait_recv()
                    if step < 3:
                        backward(wrapped, step, j).start()

                @pl.when(wrapped < y)
                def _():
                    attend(wrapped, False)

    for pair in range(heads // 2):
        at = 2 * pair * tokens
        both = acc[:, at : at + 2 * tokens]
        ratio = both[0:HD] / both[HD : HD + 1]
        stacked = jnp.concatenate([ratio[:, :tokens], ratio[:, tokens:]], axis=0)
        attn[:, pair * 128 : pair * 128 + 128] = stacked.T.astype(BF16)
    w_copy.wait()

    tiles = column_tiles(model, 768)

    def to_sibling(n):
        start, size = tiles[n]
        return push(
            part.at[1 - core, :, :, pl.ds(start, size)],
            sib.at[:, :, pl.ds(start, size)],
            s_send.at[n],
            s_recv.at[n],
            sibling,
        )

    for n, (start, size) in enumerate(tiles):
        out = jnp.dot(attn[...], w_ref[:, start : start + size], preferred_element_type=F32)
        out = out.astype(BF16)
        for d in range(2 * ZL):
            part[d % 2, d // 2, :, start : start + size] = out[d * rows : (d + 1) * rows]
        to_sibling(n).start()
    for n, (start, size) in enumerate(tiles):
        to_sibling(n).wait_recv()
        both = part[core, :, :, start : start + size].astype(F32) + sib[
            :, :, start : start + size
        ].astype(F32)
        mine[:, :, start : start + size] = both.astype(BF16)

    def to_chip(d):
        return push(
            mine.at[lax.rem(zl + d, ZL)],
            landed.at[d - 1],
            r_send.at[d - 1],
            r_recv.at[d - 1],
            l_peer[d],
        )

    for d in (2, 1, 3):
        to_chip(d).start()
    for d in (1, 3, 2):
        to_chip(d).wait_recv()
    projected = mine[zl].astype(F32)
    for d in range(ZL - 1):
        projected = projected + landed[d].astype(F32)
    attended_ref[...] = projected.astype(BF16)
    hidden = resid_ref[...].astype(F32) + projected
    square = jnp.mean(hidden * hidden, axis=-1, keepdims=True)
    payload_ref[:, 0:model] = (hidden * lax.rsqrt(square + 1e-05) * gain_ref[...]).astype(BF16)
    spare = payload_ref.shape[1] - model
    place = lax.broadcasted_iota(jnp.int32, (rows, spare), 1)
    weight = jnp.zeros((rows, spare), F32)
    for k in range(ids_ref.shape[1]):
        weight = weight + jnp.where(ids_ref[:, k : k + 1] == place % 8, rw_ref[:, k : k + 1], 0.0)
    high = weight.astype(BF16).astype(F32)
    middle = (weight - high).astype(BF16).astype(F32)
    low = weight - high - middle
    terms = jnp.where(place < 8, high, jnp.where(place < 16, middle, low))
    payload_ref[:, model:] = jnp.where(place < 24, terms, 0.0).astype(BF16)

    for j in (1, 2, 3):
        z_push(j).wait_send()
    for j in range(ZH):

        @pl.when(sends_up)
        def _():
            forward(y, 0, j).wait_send()

        @pl.when(sends_down)
        def _():
            backward(y, 0, j).wait_send()

        for step in (1, 2, 3):

            @pl.when((y - step >= 0) & sends_up)
            def _():
                forward(y - step, step, j).wait_send()

        for step in (1, 2):

            @pl.when(lax.rem(y + step, YS) <= 2)
            def _():
                backward(lax.rem(y + step, YS), step, j).wait_send()

    for n in range(len(tiles)):
        to_sibling(n).wait_send()
    for d in (1, 2, 3):
        to_chip(d).wait_send()


def attention_part(q, kv, w, resid, gain, ids, rw):
    tokens, width = q.shape
    cols = tokens * width // HD
    model = w.shape[1]
    rows = resid.shape[0]
    padded = -(-model // 128) * 128
    tiles = len(column_tiles(model, 768))
    dma = pltpu.SemaphoreType.DMA
    vmem = pl.BlockSpec(memory_space=pltpu.VMEM)
    return pl.pallas_call(
        attention_kernel,
        out_shape=(
            jax.ShapeDtypeStruct((rows, model), BF16),
            jax.ShapeDtypeStruct((rows, padded), BF16),
        ),
        in_specs=[vmem, vmem, pl.BlockSpec(memory_space=pl.ANY), vmem, vmem, vmem, vmem],
        out_specs=(vmem, vmem),
        scratch_shapes=[
            pltpu.VMEM((YS, ZH, tokens, 2 * HD), BF16),
            pltpu.VMEM((2 * HD, cols), BF16),
            pltpu.VMEM((HD + 16, ZH * tokens), BF16),
            pltpu.VMEM((1, cols), F32),
            pltpu.VMEM((HD + 16, cols), F32),
            pltpu.VMEM((tokens, width), BF16),
            pltpu.VMEM((width, model), BF16),
            pltpu.VMEM((2, ZL, rows, model), BF16),
            pltpu.VMEM((ZL, rows, model), BF16),
            pltpu.VMEM((ZL, rows, model), BF16),
            pltpu.VMEM((ZL - 1, rows, model), BF16),
            dma,
            dma,
            dma((3,)),
            dma((3,)),
            dma((4, ZH)),
            dma((4, ZH)),
            dma((3, ZH)),
            dma((3, ZH)),
            dma((tiles,)),
            dma((tiles,)),
            dma((3,)),
            dma((3,)),
        ],
        compiler_params=pltpu.CompilerParams(
            collective_id=0, has_side_effects=True, vmem_limit_bytes=VMEM_BYTES
        ),
    )(q, kv, w, resid, gain, ids, rw)


def expert_kernel(
    payload_ref,
    wgu_hbm,
    wd_hbm,
    mix_ref,
    rows_all,
    wgu,
    wd,
    made,
    from_sib,
    from_left,
    from_right,
    relay_left,
    relay_right,
    total,
    ready,
    landed,
    w_sem,
    own_sem,
    z_send,
    z_recv,
    x_send,
    x_recv,
    o_send,
    o_recv,
    s_send,
    s_recv,
    p_send,
    p_recv,
    h_send,
    h_recv,
    r_send,
    r_recv,
):
    exp = lax.axis_index("exp")
    zl, core = lax.div(exp, 2), lax.rem(exp, 2)
    x = lax.axis_index("dp")
    rows, padded = payload_ref.shape
    model = mix_ref.shape[1]
    hidden = wd.shape[0]
    left, right = lax.rem(x + XS - 1, XS), lax.rem(x + 1, XS)
    far = lax.rem(x + 2, XS)
    to_left, to_right = {"dp": left}, {"dp": right}
    sibling = {"exp": zl * 2 + 1 - core}
    l_peer = [{"exp": lax.rem(zl + d, ZL) * 2 + core} for d in range(ZL)]

    own_copy = pltpu.make_async_copy(payload_ref, rows_all.at[x, zl, core], own_sem)
    own_copy.start()
    w_copies = [
        pltpu.make_async_copy(wgu_hbm.at[0], wgu.at[0:model, 0:hidden], w_sem.at[0]),
        pltpu.make_async_copy(wgu_hbm.at[1], wgu.at[0:model, hidden : 2 * hidden], w_sem.at[1]),
        pltpu.make_async_copy(wd_hbm, wd, w_sem.at[2]),
    ]
    for copy in w_copies:
        copy.start()
    barrier_with([to_left, to_right, sibling] + l_peer[1:])

    shift = [0, 1, 3, 2]
    column = [lax.rem(zl + ZL - s, ZL) for s in shift]

    def slot(xs, j, own=False):
        return rows_all.at[xs, column[j], core]

    def z_push(j):
        return push(
            payload_ref,
            rows_all.at[x, zl, core],
            z_send.at[j - 1],
            z_recv.at[j - 1],
            l_peer[shift[j]],
        )

    def source(j):
        return payload_ref if j == 0 else slot(x, j)

    def x_push(side, j):
        return push(
            source(j), slot(x, j), x_send.at[side, j], x_recv.at[side, j], (to_right, to_left)[side]
        )

    def x_arrived(side, j):
        at = slot((left, right)[side], j)
        push(at, at, x_send.at[side, j], x_recv.at[side, j], to_right).wait_recv()

    def o_push(j):
        at = slot(left if j < 2 else right, j)
        return push(at, at, o_send.at[j], o_recv.at[j], to_right if j < 2 else to_left)

    def o_arrived(j):
        at = slot(far, j)
        push(at, at, o_send.at[j], o_recv.at[j], to_right).wait_recv()

    columns = [x, left, right, far]

    def s_push(c, j):
        src = source(j) if c == 0 else slot(columns[c], j)
        return push(src, slot(columns[c], j), s_send.at[c, j], s_recv.at[c, j], sibling)

    def s_arrived(c, j):
        at = rows_all.at[columns[c], column[j], 1 - core]
        push(at, at, s_send.at[c, j], s_recv.at[c, j], sibling).wait_recv()

    x_push(0, 0).start()
    x_push(1, 0).start()
    for j in (1, 2, 3):
        z_push(j).start()
    s_push(0, 0).start()
    wgu[model:, :] = jnp.zeros((padded - model, 2 * hidden), BF16)

    for j in (1, 2, 3):
        z_push(j).wait_recv()
        x_push(0, j).start()
        x_push(1, j).start()
        s_push(0, j).start()
        for side in (0, 1):
            x_arrived(side, j - 1)
            if (j - 1 < 2) == (side == 0):
                o_push(j - 1).start()
            s_push(1 + side, j - 1).start()
    own_copy.wait()
    for copy in w_copies:
        copy.wait()

    tiles = column_tiles(model, 768)

    def expert(c):
        for j in range(ZL):
            s_arrived(c, j)
        at = columns[c]
        inputs = rows_all[at].reshape(2 * ZL * rows, padded)
        both = jnp.dot(inputs, wgu[...], preferred_element_type=F32)
        gate, up = both[:, :hidden], both[:, hidden:]
        tail = inputs[:, padded - 128 :].astype(F32)
        place = lax.broadcasted_iota(jnp.int32, tail.shape, 1) - (128 - (padded - model))
        chosen = (place == exp) | (place == exp + 8) | (place == exp + 16)
        weight = jnp.sum(jnp.where(chosen, tail, 0.0), axis=1, keepdims=True)
        active = (gate * jax.nn.sigmoid(1.702 * gate) * (up + 1.0) * weight).astype(BF16)
        for start, size in tiles:
            out = jnp.dot(active, wd[:, start : start + size], preferred_element_type=F32)
            out = out.astype(BF16)
            for d in range(2 * ZL):
                made[at, d % 2, d // 2, :, start : start + size] = out[d * rows : (d + 1) * rows]

    def p_push(c):
        return push(
            made.at[columns[c], 1 - core],
            from_sib.at[columns[c]],
            p_send.at[c],
            p_recv.at[c],
            sibling,
        )

    def pair_sum(c):
        p_push(c).wait_recv()
        at = columns[c]
        for b in range(ZL):
            made[at, core, b] = (made[at, core, b].astype(F32) + from_sib[at, b].astype(F32)).astype(
                BF16
            )

    def half(ref, h):
        return ref.at[2 * h : 2 * h + 2]

    def h_push(n):
        src, dst, device = [
            (half(made.at[right, core], 0), half(from_left, 0), to_right),
            (half(made.at[right, core], 1), half(from_left, 1), to_right),
            (half(made.at[left, core], 0), half(from_right, 0), to_left),
            (half(made.at[left, core], 1), half(from_right, 1), to_left),
            (half(made.at[far, core], 0), relay_left, to_right),
            (half(made.at[far, core], 1), relay_right, to_left),
        ][n]
        return push(src, dst, h_send.at[n], h_recv.at[n], device)

    expert(0)
    p_push(0).start()
    for side in (0, 1):
        x_arrived(side, 3)
        if side == 1:
            o_push(3).start()
        s_push(1 + side, 3).start()
    for j in range(ZL):
        o_arrived(j)
        s_push(3, j).start()
    expert(1)
    p_push(1).start()
    expert(2)
    p_push(2).start()
    pair_sum(1)
    h_push(2).start()
    expert(3)
    p_push(3).start()
    pair_sum(2)
    h_push(1).start()
    pair_sum(3)
    h_push(4).start()
    h_push(5).start()
    pair_sum(0)
    h_push(4).wait_recv()
    for b in (0, 1):
        made[right, core, b] = (made[right, core, b].astype(F32) + relay_left[b].astype(F32)).astype(
            BF16
        )
    h_push(0).start()
    h_push(5).wait_recv()
    for b in (0, 1):
        made[left, core, 2 + b] = (
            made[left, core, 2 + b].astype(F32) + relay_right[b].astype(F32)
        ).astype(BF16)
    h_push(3).start()

    h_push(1).wait_recv()
    h_push(2).wait_recv()
    h_push(0).wait_recv()
    h_push(3).wait_recv()
    for b in range(ZL):
        summed = (
            made[x, core, b].astype(F32) + from_left[b].astype(F32) + from_right[b].astype(F32)
        )
        total[b] = summed
        ready[b] = summed.astype(BF16)

    def to_chip(d):
        return push(
            ready.at[lax.rem(zl + d, ZL)],
            landed.at[d - 1],
            r_send.at[d - 1],
            r_recv.at[d - 1],
            l_peer[d],
        )

    for d in (2, 1, 3):
        to_chip(d).start()
    for d in (1, 3, 2):
        to_chip(d).wait_recv()
    summed = total[zl]
    for d in range(ZL - 1):
        summed = summed + landed[d].astype(F32)
    mix_ref[...] = summed.astype(BF16)

    for j in (1, 2, 3):
        z_push(j).wait_send()
    for j in range(ZL):
        for side in (0, 1):
            x_push(side, j).wait_send()
        o_push(j).wait_send()
        for c in range(4):
            s_push(c, j).wait_send()
    for c in range(4):
        p_push(c).wait_send()
    for n in range(6):
        h_push(n).wait_send()
    for d in (1, 2, 3):
        to_chip(d).wait_send()


def expert_part(payload, wgu, wd):
    rows, padded = payload.shape
    hidden, model = wd.shape
    dma = pltpu.SemaphoreType.DMA
    vmem = pl.BlockSpec(memory_space=pltpu.VMEM)
    anywhere = pl.BlockSpec(memory_space=pl.ANY)
    return pl.pallas_call(
        expert_kernel,
        out_shape=jax.ShapeDtypeStruct((rows, model), BF16),
        in_specs=[vmem, anywhere, anywhere],
        out_specs=vmem,
        scratch_shapes=[
            pltpu.VMEM((XS, ZL, 2, rows, padded), BF16),
            pltpu.VMEM((padded, 2 * hidden), BF16),
            pltpu.VMEM((hidden, model), BF16),
            pltpu.VMEM((XS, 2, ZL, rows, model), BF16),
            pltpu.VMEM((XS, ZL, rows, model), BF16),
            pltpu.VMEM((ZL, rows, model), BF16),
            pltpu.VMEM((ZL, rows, model), BF16),
            pltpu.VMEM((2, rows, model), BF16),
            pltpu.VMEM((2, rows, model), BF16),
            pltpu.VMEM((ZL, rows, model), F32),
            pltpu.VMEM((ZL, rows, model), BF16),
            pltpu.VMEM((ZL - 1, rows, model), BF16),
            dma((3,)),
            dma,
            dma((3,)),
            dma((3,)),
            dma((2, ZL)),
            dma((2, ZL)),
            dma((ZL,)),
            dma((ZL,)),
            dma((4, ZL)),
            dma((4, ZL)),
            dma((4,)),
            dma((4,)),
            dma((6,)),
            dma((6,)),
            dma((3,)),
            dma((3,)),
        ],
        compiler_params=pltpu.CompilerParams(
            collective_id=1, has_side_effects=True, vmem_limit_bytes=VMEM_BYTES
        ),
    )(payload, wgu, wd)


def shards(
    queries, key_values, out_weight, resid, norm_gain, expert_ids, route_weights, w_gate_up, w_down
):
    attended, payload = attention_part(
        queries[0],
        key_values[0],
        out_weight,
        resid[0],
        norm_gain[None],
        expert_ids[0],
        route_weights[0],
    )
    mixture = expert_part(payload, w_gate_up[0], w_down[0])
    return attended[None], mixture[None]


def solution(mesh):
    return jax.shard_map(
        shards,
        mesh=mesh,
        in_specs=(
            P("dp", "ctx", "exp"),
            P("dp", "ctx", "exp"),
            P("exp", None),
            P("dp", ("ctx", "exp"), None),
            P(),
            P("dp", ("ctx", "exp"), None),
            P("dp", ("ctx", "exp"), None),
            P("exp", None, None, "dp"),
            P("exp", "dp", None),
        ),
        out_specs=(P("dp", ("ctx", "exp"), None), P("dp", ("ctx", "exp"), None)),
        check_vma=False,
    )
```

```python
import functools
import math

import jax
import jax.numpy as jnp
from jax import lax
from jax.experimental import pallas as pl
from jax.experimental.pallas import tpu as pltpu
from jax.sharding import PartitionSpec as P

HD = 64
YS = 8
ZH = 4
ZL = 4
XS = 4
MESH = pl.DeviceIdType.MESH
F32 = jnp.float32
BF16 = jnp.bfloat16
SCALE = math.log2(math.e) / math.sqrt(HD)
VMEM_BYTES = 56 * 1024 * 1024


def push(src, dst, send_sem, recv_sem, device):
    return pltpu.make_async_remote_copy(
        src_ref=src,
        dst_ref=dst,
        send_sem=send_sem,
        recv_sem=recv_sem,
        device_id=device,
        device_id_type=MESH,
    )


def column_tiles(width, step):
    return [(start, min(step, width - start)) for start in range(0, width, step)]


def barrier_with(devices):
    barrier = pltpu.get_barrier_semaphore()
    for device in devices:
        pl.semaphore_signal(barrier, inc=1, device_id=device, device_id_type=MESH)
    pl.semaphore_wait(barrier, len(devices))


def dot_t(a, b):
    return lax.dot_general(a, b, (((1,), (1,)), ((), ())), preferred_element_type=F32)


def layer_kernel(
    q_ref,
    kv_ref,
    wo_hbm,
    resid_ref,
    gain_ref,
    ids_ref,
    rw_ref,
    wgu_hbm,
    wd_hbm,
    attended_ref,
    mix_ref,
    kv_all,
    qt,
    vt,
    top,
    acc,
    attn,
    wo,
    part,
    sib,
    mine,
    landed,
    payload,
    rows_all,
    wgu,
    wd,
    made,
    from_sib,
    from_left,
    from_right,
    relay_left,
    relay_right,
    total,
    ready,
    returned,
    w_sem,
    own_sem,
    a_send,
    a_recv,
    f_send,
    f_recv,
    b_send,
    b_recv,
    e_send,
    e_recv,
    c_send,
    c_recv,
    z_send,
    z_recv,
    x_send,
    x_recv,
    o_send,
    o_recv,
    s_send,
    s_recv,
    p_send,
    p_recv,
    h_send,
    h_recv,
    r_send,
    r_recv,
):
    ctx = lax.axis_index("ctx")
    y, z = lax.div(ctx, ZH), lax.rem(ctx, ZH)
    exp = lax.axis_index("exp")
    zl, core = lax.div(exp, 2), lax.rem(exp, 2)
    x = lax.axis_index("dp")
    tokens, width = q_ref.shape
    heads = width // HD
    cols = tokens * heads
    rows, model = resid_ref.shape
    padded = payload.shape[1]
    hidden = wd.shape[1]
    tiles = column_tiles(model, 768)

    up = {"ctx": lax.rem(y + 1, YS) * ZH + z}
    down = {"ctx": lax.rem(y + YS - 1, YS) * ZH + z}
    z_peer = [{"ctx": y * ZH + lax.rem(z + d, ZH)} for d in range(ZH)]
    sibling = {"exp": zl * 2 + 1 - core}
    l_peer = [{"exp": lax.rem(zl + d, ZL) * 2 + core} for d in range(ZL)]
    left, right = lax.rem(x + XS - 1, XS), lax.rem(x + 1, XS)
    far = lax.rem(x + 2, XS)
    to_left, to_right = {"dp": left}, {"dp": right}

    w_copies = [
        pltpu.make_async_copy(wo_hbm, wo, w_sem.at[0]),
        pltpu.make_async_copy(wgu_hbm.at[0], wgu.at[0:model, 0:hidden], w_sem.at[1]),
        pltpu.make_async_copy(wgu_hbm.at[1], wgu.at[0:model, hidden : 2 * hidden], w_sem.at[2]),
        pltpu.make_async_copy(wd_hbm, wd, w_sem.at[3]),
    ]
    own_copy = pltpu.make_async_copy(kv_ref, kv_all.at[y, z], own_sem)
    own_copy.start()
    for copy in w_copies:
        copy.start()
    barrier_with([up, down, sibling, to_left, to_right] + z_peer[1:] + l_peer[1:])

    shift = [0, 1, 3, 2]
    started = []

    def gather_and_attend():
        column = [lax.rem(z + ZH - s, ZH) for s in shift]
        sends_up = y < YS - 1
        sends_down = y <= 2

        def block(group, j):
            return kv_all.at[group, column[j]]

        def forward(group, step, j):
            src = kv_ref if j == 0 and step == 0 else block(group, j)
            return push(src, block(group, j), f_send.at[step, j], f_recv.at[step, j], up)

        def backward(group, step, j):
            src = kv_ref if j == 0 and step == 0 else block(group, j)
            return push(src, block(group, j), b_send.at[step, j], b_recv.at[step, j], down)

        def z_push(j):
            return push(
                kv_ref, kv_all.at[y, z], a_send.at[j - 1], a_recv.at[j - 1], z_peer[shift[j]]
            )

        @pl.when(sends_up)
        def _():
            forward(y, 0, 0).start()

        @pl.when(sends_down)
        def _():
            backward(y, 0, 0).start()

        for j in (1, 2, 3):
            z_push(j).start()

        for pair in range(heads // 2):
            turned = q_ref[:, pair * 128 : pair * 128 + 128].astype(F32).T.astype(BF16)
            qt[0:HD, 2 * pair * tokens : (2 * pair + 1) * tokens] = turned[0:HD]
            qt[0:HD, (2 * pair + 1) * tokens : (2 * pair + 2) * tokens] = turned[HD:]
        qt[HD:, :] = jnp.zeros((128 - HD, cols), BF16)
        vt[HD:, :] = jnp.ones((vt.shape[0] - HD, vt.shape[1]), BF16)
        top[...] = jnp.full(top.shape, -1e30, F32)
        acc[...] = jnp.zeros(acc.shape, F32)
        wgu[model:, :] = jnp.zeros((padded - model, 2 * hidden), BF16)
        own_copy.wait()

        def attend(group, masked):
            for b in range(ZH):
                turned = kv_all[group, b].astype(F32).T
                vt[0:HD, b * tokens : (b + 1) * tokens] = turned[HD:].astype(BF16)
            keys = kv_all[group].reshape(ZH * tokens, 2 * HD)
            halves = [slice(0, cols // 2), slice(cols // 2, cols)]
            scores = [jnp.dot(keys, qt[:, lanes], preferred_element_type=F32) for lanes in halves]
            for lanes, seen in zip(halves, scores):
                if masked:
                    key_pos = lax.broadcasted_iota(jnp.int32, seen.shape, 0)
                    query_pos = lax.broadcasted_iota(jnp.int32, seen.shape, 1) % tokens + z * tokens
                    seen = jnp.where(key_pos <= query_pos, seen, -1e30)
                old = top[:, lanes]
                new = jnp.maximum(old, jnp.max(seen, axis=0, keepdims=True))
                probs = jnp.exp2((seen - new) * SCALE).astype(BF16)
                decay = jnp.exp2((old - new) * SCALE)
                top[:, lanes] = new
                acc[:, lanes] = acc[:, lanes] * decay + jnp.dot(
                    vt[...], probs, preferred_element_type=F32
                )

        for j in (1, 2, 3):
            z_push(j).wait_recv()

            @pl.when(sends_up)
            def _():
                forward(y, 0, j).start()

            @pl.when(sends_down)
            def _():
                backward(y, 0, j).start()

        attend(y, True)

        for step in (1, 2, 3, 4):
            group = y - step

            @pl.when(group >= 0)
            def _():
                for j in range(ZH):
                    forward(group, step - 1, j).wait_recv()
                    if step < 4:

                        @pl.when(sends_up)
                        def _():
                            forward(group, step, j).start()

                attend(group, False)

            if step < 4:
                wrapped = lax.rem(y + step, YS)

                @pl.when(wrapped <= 2)
                def _():
                    for j in range(ZH):
                        backward(wrapped, step - 1, j).wait_recv()
                        if step < 3:
                            backward(wrapped, step, j).start()

                    @pl.when(wrapped < y)
                    def _():
                        attend(wrapped, False)

        def finish():
            for j in (1, 2, 3):
                z_push(j).wait_send()
            for j in range(ZH):

                @pl.when(sends_up)
                def _():
                    forward(y, 0, j).wait_send()

                @pl.when(sends_down)
                def _():
                    backward(y, 0, j).wait_send()

                for step in (1, 2, 3):

                    @pl.when((y - step >= 0) & sends_up)
                    def _():
                        forward(y - step, step, j).wait_send()

                for step in (1, 2):

                    @pl.when(lax.rem(y + step, YS) <= 2)
                    def _():
                        backward(lax.rem(y + step, YS), step, j).wait_send()

        started.append(finish)

    def project():
        for pair in range(heads // 2):
            at = 2 * pair * tokens
            both = acc[:, at : at + 2 * tokens]
            ratio = both[0:HD] / both[HD : HD + 1]
            stacked = jnp.concatenate([ratio[:, :tokens], ratio[:, tokens:]], axis=0)
            attn[:, pair * 128 : pair * 128 + 128] = stacked.T.astype(BF16)
        w_copies[0].wait()

        def to_sibling(n):
            start, size = tiles[n]
            return push(
                part.at[1 - core, :, :, pl.ds(start, size)],
                sib.at[:, :, pl.ds(start, size)],
                e_send.at[n],
                e_recv.at[n],
                sibling,
            )

        for n, (start, size) in enumerate(tiles):
            out = dot_t(attn[...], wo[start : start + size, :]).astype(BF16)
            for d in range(2 * ZL):
                part[d % 2, d // 2, :, start : start + size] = out[d * rows : (d + 1) * rows]
            to_sibling(n).start()
        for n, (start, size) in enumerate(tiles):
            to_sibling(n).wait_recv()
            both = part[core, :, :, start : start + size].astype(F32) + sib[
                :, :, start : start + size
            ].astype(F32)
            mine[:, :, start : start + size] = both.astype(BF16)
        started.append(lambda: [to_sibling(n).wait_send() for n in range(len(tiles))])

    def sum_heads():
        def to_chip(d):
            return push(
                mine.at[lax.rem(zl + d, ZL)],
                landed.at[d - 1],
                c_send.at[d - 1],
                c_recv.at[d - 1],
                l_peer[d],
            )

        for d in (2, 1, 3):
            to_chip(d).start()
        for d in (1, 3, 2):
            to_chip(d).wait_recv()
        started.append(lambda: [to_chip(d).wait_send() for d in (1, 2, 3)])

    def norm():
        projected = mine[zl].astype(F32)
        for d in range(ZL - 1):
            projected = projected + landed[d].astype(F32)
        attended_ref[...] = projected.astype(BF16)
        state = resid_ref[...].astype(F32) + projected
        square = jnp.mean(state * state, axis=-1, keepdims=True)
        gain = gain_ref[...].reshape(1, model)
        payload[:, 0:model] = (state * lax.rsqrt(square + 1e-05) * gain).astype(BF16)
        spare = padded - model
        place = lax.broadcasted_iota(jnp.int32, (rows, spare), 1)
        same = lax.broadcasted_iota(jnp.int32, (rows, rows), 0) == lax.broadcasted_iota(
            jnp.int32, (rows, rows), 1
        )
        weight = jnp.zeros((rows, spare), F32)
        for k in range(ids_ref.shape[0]):
            named = jnp.sum(
                jnp.where(same, ids_ref[k : k + 1, :].astype(F32), 0.0), axis=1, keepdims=True
            )
            share = jnp.sum(jnp.where(same, rw_ref[k : k + 1, :], 0.0), axis=1, keepdims=True)
            weight = weight + jnp.where(named == (place % 8).astype(F32), share, 0.0)
        high = weight.astype(BF16).astype(F32)
        middle = (weight - high).astype(BF16).astype(F32)
        low = weight - high - middle
        terms = jnp.where(place < 8, high, jnp.where(place < 16, middle, low))
        payload[:, model:] = jnp.where(place < 24, terms, 0.0).astype(BF16)

    column = [lax.rem(zl + ZL - s, ZL) for s in shift]
    columns = [x, left, right, far]

    def slot(at, j):
        return rows_all.at[at, column[j], core]

    def expert(c):
        at = columns[c]
        inputs = rows_all[at].reshape(2 * ZL * rows, padded)
        both = jnp.dot(inputs, wgu[...], preferred_element_type=F32)
        gate, upper = both[:, :hidden], both[:, hidden:]
        tail = inputs[:, padded - 128 :].astype(F32)
        place = lax.broadcasted_iota(jnp.int32, tail.shape, 1) - (128 - (padded - model))
        chosen = (place == exp) | (place == exp + 8) | (place == exp + 16)
        weight = jnp.sum(jnp.where(chosen, tail, 0.0), axis=1, keepdims=True)
        active = (gate * jax.nn.sigmoid(1.702 * gate) * (upper + 1.0) * weight).astype(BF16)
        for start, size in tiles:
            out = dot_t(active, wd[start : start + size, :]).astype(BF16)
            for d in range(2 * ZL):
                made[at, d % 2, d // 2, :, start : start + size] = out[d * rows : (d + 1) * rows]

    def p_push(c):
        return push(
            made.at[columns[c], 1 - core],
            from_sib.at[columns[c]],
            p_send.at[c],
            p_recv.at[c],
            sibling,
        )

    def gather_and_apply():
        def z_push(j):
            return push(
                payload,
                rows_all.at[x, zl, core],
                z_send.at[j - 1],
                z_recv.at[j - 1],
                l_peer[shift[j]],
            )

        def source(j):
            return payload if j == 0 else slot(x, j)

        def x_push(side, j):
            device = (to_right, to_left)[side]
            return push(source(j), slot(x, j), x_send.at[side, j], x_recv.at[side, j], device)

        def x_arrived(side, j):
            at = slot((left, right)[side], j)
            push(at, at, x_send.at[side, j], x_recv.at[side, j], to_right).wait_recv()

        def o_push(j):
            at = slot(left if j < 2 else right, j)
            return push(at, at, o_send.at[j], o_recv.at[j], to_right if j < 2 else to_left)

        def o_arrived(j):
            at = slot(far, j)
            push(at, at, o_send.at[j], o_recv.at[j], to_right).wait_recv()

        def s_push(c, j):
            src = source(j) if c == 0 else slot(columns[c], j)
            return push(src, slot(columns[c], j), s_send.at[c, j], s_recv.at[c, j], sibling)

        def s_arrived(c, j):
            at = rows_all.at[columns[c], column[j], 1 - core]
            push(at, at, s_send.at[c, j], s_recv.at[c, j], sibling).wait_recv()

        own = pltpu.make_async_copy(payload, rows_all.at[x, zl, core], own_sem)
        own.start()
        x_push(0, 0).start()
        x_push(1, 0).start()
        for j in (1, 2, 3):
            z_push(j).start()
        s_push(0, 0).start()
        for j in (1, 2, 3):
            z_push(j).wait_recv()
            x_push(0, j).start()
            x_push(1, j).start()
            s_push(0, j).start()
            for side in (0, 1):
                x_arrived(side, j - 1)
                if (j - 1 < 2) == (side == 0):
                    o_push(j - 1).start()
                s_push(1 + side, j - 1).start()
        own.wait()
        for copy in w_copies[1:]:
            copy.wait()
        for j in range(ZL):
            s_arrived(0, j)
        expert(0)
        p_push(0).start()
        for side in (0, 1):
            x_arrived(side, 3)
            if side == 1:
                o_push(3).start()
            s_push(1 + side, 3).start()
        for j in range(ZL):
            o_arrived(j)
            s_push(3, j).start()
        for c in (1, 2, 3):
            for j in range(ZL):
                s_arrived(c, j)
            expert(c)
            p_push(c).start()

        def finish():
            for j in (1, 2, 3):
                z_push(j).wait_send()
            for j in range(ZL):
                for side in (0, 1):
                    x_push(side, j).wait_send()
                o_push(j).wait_send()
                for c in range(4):
                    s_push(c, j).wait_send()
            for c in range(4):
                p_push(c).wait_send()

        started.append(finish)

    def sum_columns():
        def pair_sum(c):
            p_push(c).wait_recv()
            at = columns[c]
            for b in range(ZL):
                made[at, core, b] = (
                    made[at, core, b].astype(F32) + from_sib[at, b].astype(F32)
                ).astype(BF16)

        def half(ref, h):
            return ref.at[2 * h : 2 * h + 2]

        def h_push(n):
            src, dst, device = [
                (half(made.at[right, core], 0), half(from_left, 0), to_right),
                (half(made.at[right, core], 1), half(from_left, 1), to_right),
                (half(made.at[left, core], 0), half(from_right, 0), to_left),
                (half(made.at[left, core], 1), half(from_right, 1), to_left),
                (half(made.at[far, core], 0), relay_left, to_right),
                (half(made.at[far, core], 1), relay_right, to_left),
            ][n]
            return push(src, dst, h_send.at[n], h_recv.at[n], device)

        pair_sum(1)
        h_push(2).start()
        pair_sum(2)
        h_push(1).start()
        pair_sum(3)
        h_push(4).start()
        h_push(5).start()
        pair_sum(0)
        h_push(4).wait_recv()
        for b in (0, 1):
            made[right, core, b] = (
                made[right, core, b].astype(F32) + relay_left[b].astype(F32)
            ).astype(BF16)
        h_push(0).start()
        h_push(5).wait_recv()
        for b in (0, 1):
            made[left, core, 2 + b] = (
                made[left, core, 2 + b].astype(F32) + relay_right[b].astype(F32)
            ).astype(BF16)
        h_push(3).start()
        for n in (1, 2, 0, 3):
            h_push(n).wait_recv()
        started.append(lambda: [h_push(n).wait_send() for n in range(6)])

    def sum_slices():
        for b in range(ZL):
            summed = (
                made[x, core, b].astype(F32) + from_left[b].astype(F32) + from_right[b].astype(F32)
            )
            total[b] = summed
            ready[b] = summed.astype(BF16)

        def to_chip(d):
            return push(
                ready.at[lax.rem(zl + d, ZL)],
                returned.at[d - 1],
                r_send.at[d - 1],
                r_recv.at[d - 1],
                l_peer[d],
            )

        for d in (2, 1, 3):
            to_chip(d).start()
        for d in (1, 3, 2):
            to_chip(d).wait_recv()
        summed = total[zl]
        for d in range(ZL - 1):
            summed = summed + returned[d].astype(F32)
        mix_ref[...] = summed.astype(BF16)
        started.append(lambda: [to_chip(d).wait_send() for d in (1, 2, 3)])

    gather_and_attend()
    project()
    sum_heads()
    norm()
    gather_and_apply()
    sum_columns()
    sum_slices()
    for finish in started:
        finish()


def layer(q, kv, wo, resid, gain, ids, rw, wgu, wd):
    tokens, width = q.shape
    cols = tokens * width // HD
    rows, model = resid.shape
    hidden = wd.shape[1]
    padded = -(-model // 128) * 128
    tiles = len(column_tiles(model, 768))
    dma = pltpu.SemaphoreType.DMA
    vmem = pl.BlockSpec(memory_space=pltpu.VMEM)
    hbm = pl.BlockSpec(memory_space=pl.ANY)
    return pl.pallas_call(
        layer_kernel,
        out_shape=(
            jax.ShapeDtypeStruct((rows, model), BF16),
            jax.ShapeDtypeStruct((rows, model), BF16),
        ),
        in_specs=[vmem, vmem, hbm, vmem, vmem, vmem, vmem, hbm, hbm],
        out_specs=(vmem, vmem),
        scratch_shapes=[
            pltpu.VMEM((YS, ZH, tokens, 2 * HD), BF16),
            pltpu.VMEM((2 * HD, cols), BF16),
            pltpu.VMEM((HD + 16, ZH * tokens), BF16),
            pltpu.VMEM((1, cols), F32),
            pltpu.VMEM((HD + 16, cols), F32),
            pltpu.VMEM((tokens, width), BF16),
            pltpu.VMEM((model, width), BF16),
            pltpu.VMEM((2, ZL, rows, model), BF16),
            pltpu.VMEM((ZL, rows, model), BF16),
            pltpu.VMEM((ZL, rows, model), BF16),
            pltpu.VMEM((ZL - 1, rows, model), BF16),
            pltpu.VMEM((rows, padded), BF16),
            pltpu.VMEM((XS, ZL, 2, rows, padded), BF16),
            pltpu.VMEM((padded, 2 * hidden), BF16),
            pltpu.VMEM((model, hidden), BF16),
            pltpu.VMEM((XS, 2, ZL, rows, model), BF16),
            pltpu.VMEM((XS, ZL, rows, model), BF16),
            pltpu.VMEM((ZL, rows, model), BF16),
            pltpu.VMEM((ZL, rows, model), BF16),
            pltpu.VMEM((2, rows, model), BF16),
            pltpu.VMEM((2, rows, model), BF16),
            pltpu.VMEM((ZL, rows, model), F32),
            pltpu.VMEM((ZL, rows, model), BF16),
            pltpu.VMEM((ZL - 1, rows, model), BF16),
            dma((4,)),
            dma,
        ]
        + [dma((3,))] * 2
        + [dma((4, ZH))] * 2
        + [dma((3, ZH))] * 2
        + [dma((tiles,))] * 2
        + [dma((3,))] * 2
        + [dma((3,))] * 2
        + [dma((2, ZL))] * 2
        + [dma((ZL,))] * 2
        + [dma((4, ZL))] * 2
        + [dma((4,))] * 2
        + [dma((6,))] * 2
        + [dma((3,))] * 2,
        compiler_params=pltpu.CompilerParams(
            collective_id=0, has_side_effects=True, vmem_limit_bytes=VMEM_BYTES
        ),
    )(q, kv, wo, resid, gain, ids, rw, wgu, wd)


def shards(
    queries, key_values, out_weight, resid, norm_gain, expert_ids, route_weights, w_gate_up, w_down
):
    attended, mixture = layer(
        queries[0],
        key_values[0],
        out_weight.T,
        resid[0],
        norm_gain,
        expert_ids[0].T,
        route_weights[0].T,
        w_gate_up[0],
        w_down[0].T,
    )
    return attended[None], mixture[None]


def solution(mesh):
    return jax.shard_map(
        shards,
        mesh=mesh,
        in_specs=(
            P("dp", "ctx", "exp"),
            P("dp", "ctx", "exp"),
            P("exp", None),
            P("dp", ("ctx", "exp"), None),
            P(),
            P("dp", ("ctx", "exp"), None),
            P("dp", ("ctx", "exp"), None),
            P("exp", None, None, "dp"),
            P("exp", "dp", None),
        ),
        out_specs=(P("dp", ("ctx", "exp"), None), P("dp", ("ctx", "exp"), None)),
        check_vma=False,
    )
```

```python
import functools
import math

import jax
import jax.numpy as jnp
from jax import lax
from jax.experimental import pallas as pl
from jax.experimental.pallas import tpu as pltpu
from jax.sharding import PartitionSpec as P

HD = 64
YS = 8
ZH = 4
ZL = 4
XS = 4
MESH = pl.DeviceIdType.MESH
F32 = jnp.float32
BF16 = jnp.bfloat16
SCALE = math.log2(math.e) / math.sqrt(HD)
VMEM_BYTES = 56 * 1024 * 1024


def push(src, dst, send_sem, recv_sem, device):
    return pltpu.make_async_remote_copy(
        src_ref=src,
        dst_ref=dst,
        send_sem=send_sem,
        recv_sem=recv_sem,
        device_id=device,
        device_id_type=MESH,
    )


def column_tiles(width, step):
    return [(start, min(step, width - start)) for start in range(0, width, step)]


def column_pieces(model, padded):
    cut = padded // 256 * 128
    tiles = column_tiles(cut, 768) + [(cut + a, b) for a, b in column_tiles(model - cut, 768)]
    return [(0, cut), (cut, padded - cut)], tiles


def barrier_with(devices):
    barrier = pltpu.get_barrier_semaphore()
    for device in devices:
        pl.semaphore_signal(barrier, inc=1, device_id=device, device_id_type=MESH)
    pl.semaphore_wait(barrier, len(devices))


def dot_t(a, b):
    return lax.dot_general(a, b, (((1,), (1,)), ((), ())), preferred_element_type=F32)


def layer_kernel(
    q_ref,
    kv_ref,
    wo_hbm,
    resid_ref,
    gain_ref,
    ids_ref,
    rw_ref,
    wgu_hbm,
    wd_hbm,
    attended_ref,
    mix_ref,
    kv_all,
    qt,
    vt,
    top,
    acc,
    attn,
    wo,
    part,
    sib,
    mine,
    landed,
    payload,
    rows_all,
    wgu,
    wd,
    made,
    from_sib,
    from_left,
    from_right,
    relays,
    total,
    ready,
    returned,
    w_sem,
    own_sem,
    a_send,
    a_recv,
    f_send,
    f_recv,
    b_send,
    b_recv,
    e_send,
    e_recv,
    c_send,
    c_recv,
    z_send,
    z_recv,
    x_send,
    x_recv,
    o_send,
    o_recv,
    s_send,
    s_recv,
    t_send,
    t_recv,
    p_send,
    p_recv,
    g_send,
    g_recv,
    k_send,
    k_recv,
    h_send,
    h_recv,
    r_send,
    r_recv,
):
    ctx = lax.axis_index("ctx")
    y, z = lax.div(ctx, ZH), lax.rem(ctx, ZH)
    exp = lax.axis_index("exp")
    zl, core = lax.div(exp, 2), lax.rem(exp, 2)
    x = lax.axis_index("dp")
    tokens, width = q_ref.shape
    heads = width // HD
    cols = tokens * heads
    rows, model = resid_ref.shape
    padded = payload.shape[1]
    hidden = wd.shape[1]
    pieces, tiles = column_pieces(model, padded)

    up = {"ctx": lax.rem(y + 1, YS) * ZH + z}
    down = {"ctx": lax.rem(y + YS - 1, YS) * ZH + z}
    z_peer = [{"ctx": y * ZH + lax.rem(z + d, ZH)} for d in range(ZH)]
    sibling = {"exp": zl * 2 + 1 - core}
    l_peer = [{"exp": lax.rem(zl + d, ZL) * 2 + core} for d in range(ZL)]
    left, right = lax.rem(x + XS - 1, XS), lax.rem(x + 1, XS)
    far = lax.rem(x + 2, XS)
    to_left, to_right = {"dp": left}, {"dp": right}

    w_copies = [
        pltpu.make_async_copy(wo_hbm, wo, w_sem.at[0]),
        pltpu.make_async_copy(wgu_hbm.at[0], wgu.at[0:model, 0:hidden], w_sem.at[1]),
        pltpu.make_async_copy(wgu_hbm.at[1], wgu.at[0:model, hidden : 2 * hidden], w_sem.at[2]),
        pltpu.make_async_copy(wd_hbm, wd, w_sem.at[3]),
    ]
    own_copy = pltpu.make_async_copy(kv_ref, kv_all.at[y, z], own_sem)
    own_copy.start()
    for copy in w_copies:
        copy.start()
    barrier_with([up, down, sibling, to_left, to_right] + z_peer[1:] + l_peer[1:])

    shift = [0, 1, 3, 2]
    started = []

    def gather_and_attend():
        column = [lax.rem(z + ZH - s, ZH) for s in shift]
        sends_up = y < YS - 1
        sends_down = y <= 2

        def block(group, j):
            return kv_all.at[group, column[j]]

        def forward(group, step, j):
            src = kv_ref if j == 0 and step == 0 else block(group, j)
            return push(src, block(group, j), f_send.at[step, j], f_recv.at[step, j], up)

        def backward(group, step, j):
            src = kv_ref if j == 0 and step == 0 else block(group, j)
            return push(src, block(group, j), b_send.at[step, j], b_recv.at[step, j], down)

        def z_push(j):
            return push(
                kv_ref, kv_all.at[y, z], a_send.at[j - 1], a_recv.at[j - 1], z_peer[shift[j]]
            )

        @pl.when(sends_up)
        def _():
            forward(y, 0, 0).start()

        @pl.when(sends_down)
        def _():
            backward(y, 0, 0).start()

        for j in (1, 2, 3):
            z_push(j).start()

        for pair in range(heads // 2):
            turned = q_ref[:, pair * 128 : pair * 128 + 128].astype(F32).T.astype(BF16)
            qt[0:HD, 2 * pair * tokens : (2 * pair + 1) * tokens] = turned[0:HD]
            qt[0:HD, (2 * pair + 1) * tokens : (2 * pair + 2) * tokens] = turned[HD:]
        qt[HD:, :] = jnp.zeros((128 - HD, cols), BF16)
        vt[HD:, :] = jnp.ones((vt.shape[0] - HD, vt.shape[1]), BF16)
        top[...] = jnp.full(top.shape, -1e30, F32)
        acc[...] = jnp.zeros(acc.shape, F32)
        wgu[model:, :] = jnp.zeros((padded - model, 2 * hidden), BF16)
        own_copy.wait()

        def attend(group, masked):
            for b in range(ZH):
                turned = kv_all[group, b].astype(F32).T
                vt[0:HD, b * tokens : (b + 1) * tokens] = turned[HD:].astype(BF16)
            keys = kv_all[group].reshape(ZH * tokens, 2 * HD)
            halves = [slice(0, cols // 2), slice(cols // 2, cols)]
            scores = [jnp.dot(keys, qt[:, lanes], preferred_element_type=F32) for lanes in halves]
            for lanes, seen in zip(halves, scores):
                if masked:
                    key_pos = lax.broadcasted_iota(jnp.int32, seen.shape, 0)
                    query_pos = lax.broadcasted_iota(jnp.int32, seen.shape, 1) % tokens + z * tokens
                    seen = jnp.where(key_pos <= query_pos, seen, -1e30)
                old = top[:, lanes]
                new = jnp.maximum(old, jnp.max(seen, axis=0, keepdims=True))
                probs = jnp.exp2((seen - new) * SCALE).astype(BF16)
                decay = jnp.exp2((old - new) * SCALE)
                top[:, lanes] = new
                acc[:, lanes] = acc[:, lanes] * decay + jnp.dot(
                    vt[...], probs, preferred_element_type=F32
                )

        for j in (1, 2, 3):
            z_push(j).wait_recv()

            @pl.when(sends_up)
            def _():
                forward(y, 0, j).start()

            @pl.when(sends_down)
            def _():
                backward(y, 0, j).start()

        attend(y, True)

        for step in (1, 2, 3, 4):
            group = y - step

            @pl.when(group >= 0)
            def _():
                for j in range(ZH):
                    forward(group, step - 1, j).wait_recv()
                    if step < 4:

                        @pl.when(sends_up)
                        def _():
                            forward(group, step, j).start()

                attend(group, False)

            if step < 4:
                wrapped = lax.rem(y + step, YS)

                @pl.when(wrapped <= 2)
                def _():
                    for j in range(ZH):
                        backward(wrapped, step - 1, j).wait_recv()
                        if step < 3:
                            backward(wrapped, step, j).start()

                    @pl.when(wrapped < y)
                    def _():
                        attend(wrapped, False)

        def finish():
            for j in (1, 2, 3):
                z_push(j).wait_send()
            for j in range(ZH):

                @pl.when(sends_up)
                def _():
                    forward(y, 0, j).wait_send()

                @pl.when(sends_down)
                def _():
                    backward(y, 0, j).wait_send()

                for step in (1, 2, 3):

                    @pl.when((y - step >= 0) & sends_up)
                    def _():
                        forward(y - step, step, j).wait_send()

                for step in (1, 2):

                    @pl.when(lax.rem(y + step, YS) <= 2)
                    def _():
                        backward(lax.rem(y + step, YS), step, j).wait_send()

        started.append(finish)

    def project():
        for pair in range(heads // 2):
            at = 2 * pair * tokens
            both = acc[:, at : at + 2 * tokens]
            ratio = both[0:HD] / both[HD : HD + 1]
            stacked = jnp.concatenate([ratio[:, :tokens], ratio[:, tokens:]], axis=0)
            attn[:, pair * 128 : pair * 128 + 128] = stacked.T.astype(BF16)
        w_copies[0].wait()

        def to_sibling(n):
            start, size = tiles[n]
            return push(
                part.at[1 - core, :, :, pl.ds(start, size)],
                sib.at[:, :, pl.ds(start, size)],
                e_send.at[n],
                e_recv.at[n],
                sibling,
            )

        for n, (start, size) in enumerate(tiles):
            out = dot_t(attn[...], wo[start : start + size, :]).astype(BF16)
            for d in range(2 * ZL):
                part[d % 2, d // 2, :, start : start + size] = out[d * rows : (d + 1) * rows]
            to_sibling(n).start()
        for n, (start, size) in enumerate(tiles):
            to_sibling(n).wait_recv()
            both = part[core, :, :, start : start + size].astype(F32) + sib[
                :, :, start : start + size
            ].astype(F32)
            mine[:, :, start : start + size] = both.astype(BF16)
            for piece in (0, 1):
                if start + size == min(sum(pieces[piece]), model):
                    for j in (1, 2, 3):
                        to_chip(j, piece).start()
        started.append(lambda: [to_sibling(n).wait_send() for n in range(len(tiles))])
        started.append(
            lambda: [to_chip(j, piece).wait_send() for j in (1, 2, 3) for piece in (0, 1)]
        )

    def model_columns(piece):
        start, size = pieces[piece]
        return start, min(size, model - start)

    def to_chip(j, piece):
        lanes = pl.ds(*model_columns(piece))
        return push(
            mine.at[column[j], :, lanes],
            landed.at[zl, :, lanes],
            c_send.at[piece, j - 1],
            c_recv.at[piece, zl],
            {"exp": column[j] * 2 + core},
        )

    def finish_rows(piece, square):
        start, size = model_columns(piece)
        lanes = slice(start, start + size)
        projected = mine[zl, :, lanes].astype(F32)
        for j in (1, 2, 3):
            at = landed.at[column[j], :, pl.ds(start, size)]
            push(at, at, c_send.at[piece, 0], c_recv.at[piece, column[j]], sibling).wait_recv()
            projected = projected + landed[column[j], :, lanes].astype(F32)
        attended_ref[:, lanes] = projected.astype(BF16)
        state = resid_ref[:, lanes].astype(F32) + projected
        gain = gain_ref[lanes].reshape(1, size)
        payload[:, lanes] = (state * gain).astype(BF16)
        return square + jnp.sum(state * state, axis=-1, keepdims=True)

    def finish_tail(square):
        spare = padded - model
        place = lax.broadcasted_iota(jnp.int32, (rows, spare), 1)
        same = lax.broadcasted_iota(jnp.int32, (rows, rows), 0) == lax.broadcasted_iota(
            jnp.int32, (rows, rows), 1
        )
        weight = jnp.zeros((rows, spare), F32)
        for k in range(ids_ref.shape[0]):
            named = jnp.sum(
                jnp.where(same, ids_ref[k : k + 1, :].astype(F32), 0.0), axis=1, keepdims=True
            )
            share = jnp.sum(jnp.where(same, rw_ref[k : k + 1, :], 0.0), axis=1, keepdims=True)
            weight = weight + jnp.where(named == (place % 9).astype(F32), share, 0.0)
        inverse = lax.rsqrt(square / model + 1e-05)
        weight = jnp.where(place % 9 == 8, inverse, weight)
        high = weight.astype(BF16).astype(F32)
        middle = (weight - high).astype(BF16).astype(F32)
        low = weight - high - middle
        terms = jnp.where(place < 9, high, jnp.where(place < 18, middle, low))
        payload[:, model:] = jnp.where(place < 27, terms, 0.0).astype(BF16)

    side = lax.div(zl, 2)
    place_in = zl + side * (ZL - 1 - 2 * zl)
    column = [zl]
    for j in range(1, ZL):
        at = j - 1 + lax.div(j - 1 + ZL - place_in, ZL)
        column.append(at + side * (ZL - 1 - 2 * at))
    columns = [x, left, right, far]

    def slot(at, j, piece):
        return rows_all.at[at, core, column[j], :, pl.ds(*pieces[piece])]

    def expert(c):
        at = columns[c]
        inputs = rows_all[at].reshape(2 * ZL * rows, padded)
        both = jnp.dot(inputs, wgu[...], preferred_element_type=F32)
        tail = inputs[:, padded - 128 :].astype(F32)
        place = lax.broadcasted_iota(jnp.int32, tail.shape, 1) - (128 - (padded - model))

        def terms_of(n):
            chosen = (place == n) | (place == n + 9) | (place == n + 18)
            return jnp.sum(jnp.where(chosen, tail, 0.0), axis=1, keepdims=True)

        weight, inverse = terms_of(exp), terms_of(8)
        gate, upper = both[:, :hidden] * inverse, both[:, hidden:] * inverse
        active = (gate * jax.nn.sigmoid(1.702 * gate) * (upper + 1.0) * weight).astype(BF16)
        for start, size in column_tiles(model, 768):
            out = dot_t(active, wd[start : start + size, :]).astype(BF16)
            for d in range(2 * ZL):
                made[at, d // ZL, d % ZL, :, start : start + size] = out[d * rows : (d + 1) * rows]

    def p_push(c):
        return push(
            made.at[columns[c], 1 - core],
            from_sib.at[columns[c]],
            p_send.at[c],
            p_recv.at[c],
            sibling,
        )

    def pair_sum(c):
        p_push(c).wait_recv()
        at = columns[c]
        for b in range(ZL):
            made[at, core, b] = (made[at, core, b].astype(F32) + from_sib[at, b].astype(F32)).astype(
                BF16
            )

    def to_right_column(b):
        src = made.at[right, core, b]
        return push(src, from_left.at[b], g_send.at[b], g_recv.at[b], to_right)

    def to_left_column(b):
        src = made.at[left, core, b]
        return push(src, from_right.at[b], h_send.at[b], h_recv.at[b], to_left)

    def relay(b):
        src = made.at[far, core, b]
        dst = relays.at[b]
        return push(src, dst, k_send.at[b], k_recv.at[b], to_right if b < 2 else to_left)

    def gather_and_apply():
        def z_push(j, p):
            return push(
                source(0, p),
                slot(x, 0, p),
                z_send.at[p, j - 1],
                z_recv.at[p, zl],
                {"exp": column[j] * 2 + core},
            )

        def z_arrived(j, p):
            at = slot(x, j, p)
            push(at, at, z_send.at[p, j - 1], z_recv.at[p, column[j]], sibling).wait_recv()

        def source(j, p):
            return payload.at[:, pl.ds(*pieces[p])] if j == 0 else slot(x, j, p)

        def x_push(way, j, p):
            device = (to_right, to_left)[way]
            return push(
                source(j, p), slot(x, j, p), x_send.at[p, way, j], x_recv.at[p, way, j], device
            )

        def x_arrived(way, j, p):
            at = slot((left, right)[way], j, p)
            push(at, at, x_send.at[p, way, j], x_recv.at[p, way, j], to_right).wait_recv()

        def o_push(j, p):
            at = slot(left if j < 2 else right, j, p)
            return push(at, at, o_send.at[p, j], o_recv.at[p, j], to_right if j < 2 else to_left)

        def o_arrived(j, p):
            at = slot(far, j, p)
            push(at, at, o_send.at[p, j], o_recv.at[p, j], to_right).wait_recv()

        def s_push(c):
            at = rows_all.at[columns[c], core]
            return push(at, at, s_send.at[c], s_recv.at[c], sibling)

        def s_arrived(c):
            at = rows_all.at[columns[c], 1 - core]
            push(at, at, s_send.at[c], s_recv.at[c], sibling).wait_recv()

        def t_push(j):
            at = rows_all.at[far, core, column[j]]
            return push(at, at, t_send.at[j], t_recv.at[j], sibling)

        def t_arrived(j):
            at = rows_all.at[far, 1 - core, column[j]]
            push(at, at, t_send.at[j], t_recv.at[j], sibling).wait_recv()

        def start_rows(p):
            x_push(0, 0, p).start()
            x_push(1, 0, p).start()
            for j in (1, 2, 3):
                z_push(j, p).start()

        def z_forward(j, p):
            z_arrived(j, p)
            x_push(0, j, p).start()
            x_push(1, j, p).start()

        def x_forward(j, p):
            for way in (0, 1):
                x_arrived(way, j, p)
                if (j < 2) == (way == 0):
                    o_push(j, p).start()

        square = finish_rows(0, jnp.zeros((rows, 1), F32))
        start_rows(0)
        finish_tail(finish_rows(1, square))
        start_rows(1)
        own = pltpu.make_async_copy(payload, rows_all.at[x, core, zl], own_sem)
        own.start()
        x_forward(0, 0)
        z_forward(1, 0)
        x_forward(0, 1)
        z_forward(2, 0)
        x_forward(1, 0)
        z_forward(3, 0)
        x_forward(2, 0)
        z_forward(1, 1)
        x_forward(3, 0)
        z_forward(2, 1)
        x_forward(1, 1)
        z_forward(3, 1)
        own.wait()
        s_push(0).start()
        x_forward(2, 1)
        x_forward(3, 1)
        s_push(1).start()
        s_push(2).start()
        for copy in w_copies[1:]:
            copy.wait()
        s_arrived(1)
        expert(1)
        p_push(1).start()
        for j in range(ZL):
            o_arrived(j, 0)
            if j < 2:
                o_arrived(j, 1)
                t_push(j).start()
        s_arrived(2)
        expert(2)
        p_push(2).start()
        for j in (2, 3):
            o_arrived(j, 1)
            t_push(j).start()
        pair_sum(1)
        to_left_column(0).start()
        to_left_column(1).start()
        pair_sum(2)
        to_right_column(3).start()
        to_right_column(2).start()
        for j in range(ZL):
            t_arrived(j)
        expert(3)
        p_push(3).start()
        s_arrived(0)
        pair_sum(3)
        for b in (0, 1):
            relay(b).start()
            relay(3 - b).start()
        expert(0)
        p_push(0).start()

        def finish():
            for p in (0, 1):
                for j in (1, 2, 3):
                    z_push(j, p).wait_send()
                for j in range(ZL):
                    for way in (0, 1):
                        x_push(way, j, p).wait_send()
                    o_push(j, p).wait_send()
            for c in range(4):
                p_push(c).wait_send()
                t_push(c).wait_send()
                if c < 3:
                    s_push(c).wait_send()

        started.append(finish)

    def sum_columns():
        for b in (0, 3, 1, 2):
            relay(b).wait_recv()
            at = right if b < 2 else left
            made[at, core, b] = (made[at, core, b].astype(F32) + relays[b].astype(F32)).astype(BF16)
            if b < 2:
                to_right_column(b).start()
            else:
                to_left_column(b).start()
        pair_sum(0)

        def to_chip(b):
            return push(
                ready.at[b],
                returned.at[zl],
                r_send.at[b],
                r_recv.at[zl],
                {"exp": b * 2 + core},
            )

        for b in (0, 3, 1, 2):
            to_right_column(b).wait_recv()
            to_left_column(b).wait_recv()
            summed = (
                made[x, core, b].astype(F32) + from_left[b].astype(F32) + from_right[b].astype(F32)
            )
            total[b] = summed
            ready[b] = summed.astype(BF16)

            @pl.when(zl != b)
            def _():
                to_chip(b).start()

        mix = total[zl]
        for j in range(1, ZL):
            at = returned.at[column[j]]
            push(at, at, r_send.at[j], r_recv.at[column[j]], sibling).wait_recv()
            mix = mix + returned[column[j]].astype(F32)
        mix_ref[...] = mix.astype(BF16)

        def finish():
            for b in range(ZL):
                to_right_column(b).wait_send()
                to_left_column(b).wait_send()
                relay(b).wait_send()

                @pl.when(zl != b)
                def _():
                    to_chip(b).wait_send()

        started.append(finish)

    gather_and_attend()
    project()
    gather_and_apply()
    sum_columns()
    for finish in started:
        finish()


def layer(q, kv, wo, resid, gain, ids, rw, wgu, wd):
    tokens, width = q.shape
    cols = tokens * width // HD
    rows, model = resid.shape
    hidden = wd.shape[1]
    padded = -(-model // 128) * 128
    tiles = len(column_pieces(model, padded)[1])
    dma = pltpu.SemaphoreType.DMA
    vmem = pl.BlockSpec(memory_space=pltpu.VMEM)
    hbm = pl.BlockSpec(memory_space=pl.ANY)
    return pl.pallas_call(
        layer_kernel,
        out_shape=(
            jax.ShapeDtypeStruct((rows, model), BF16),
            jax.ShapeDtypeStruct((rows, model), BF16),
        ),
        in_specs=[vmem, vmem, hbm, vmem, vmem, vmem, vmem, hbm, hbm],
        out_specs=(vmem, vmem),
        scratch_shapes=[
            pltpu.VMEM((YS, ZH, tokens, 2 * HD), BF16),
            pltpu.VMEM((2 * HD, cols), BF16),
            pltpu.VMEM((HD + 16, ZH * tokens), BF16),
            pltpu.VMEM((1, cols), F32),
            pltpu.VMEM((HD + 16, cols), F32),
            pltpu.VMEM((tokens, width), BF16),
            pltpu.VMEM((model, width), BF16),
            pltpu.VMEM((2, ZL, rows, model), BF16),
            pltpu.VMEM((ZL, rows, model), BF16),
            pltpu.VMEM((ZL, rows, model), BF16),
            pltpu.VMEM((ZL, rows, model), BF16),
            pltpu.VMEM((rows, padded), BF16),
            pltpu.VMEM((XS, 2, ZL, rows, padded), BF16),
            pltpu.VMEM((padded, 2 * hidden), BF16),
            pltpu.VMEM((model, hidden), BF16),
            pltpu.VMEM((XS, 2, ZL, rows, model), BF16),
            pltpu.VMEM((XS, ZL, rows, model), BF16),
            pltpu.VMEM((ZL, rows, model), BF16),
            pltpu.VMEM((ZL, rows, model), BF16),
            pltpu.VMEM((ZL, rows, model), BF16),
            pltpu.VMEM((ZL, rows, model), F32),
            pltpu.VMEM((ZL, rows, model), BF16),
            pltpu.VMEM((ZL, rows, model), BF16),
            dma((4,)),
            dma,
        ]
        + [dma((ZH,))] * 2
        + [dma((4, ZH))] * 2
        + [dma((3, ZH))] * 2
        + [dma((tiles,))] * 2
        + [dma((2, ZL))] * 2
        + [dma((2, ZL))] * 2
        + [dma((2, 2, ZL))] * 2
        + [dma((2, ZL))] * 2
        + [dma((3,))] * 2
        + [dma((ZL,))] * 2
        + [dma((4,))] * 2
        + [dma((ZL,))] * 8,
        compiler_params=pltpu.CompilerParams(
            collective_id=0, has_side_effects=True, vmem_limit_bytes=VMEM_BYTES
        ),
    )(q, kv, wo, resid, gain, ids, rw, wgu, wd)


def shards(
    queries, key_values, out_weight, resid, norm_gain, expert_ids, route_weights, w_gate_up, w_down
):
    attended, mixture = layer(
        queries[0],
        key_values[0],
        out_weight.T,
        resid[0],
        norm_gain,
        expert_ids[0].T,
        route_weights[0].T,
        w_gate_up[0],
        w_down[0].T,
    )
    return attended[None], mixture[None]


def solution(mesh):
    return jax.shard_map(
        shards,
        mesh=mesh,
        in_specs=(
            P("dp", "ctx", "exp"),
            P("dp", "ctx", "exp"),
            P("exp", None),
            P("dp", ("ctx", "exp"), None),
            P(),
            P("dp", ("ctx", "exp"), None),
            P("dp", ("ctx", "exp"), None),
            P("exp", None, None, "dp"),
            P("exp", "dp", None),
        ),
        out_specs=(P("dp", ("ctx", "exp"), None), P("dp", ("ctx", "exp"), None)),
        check_vma=False,
    )
```

```python
import functools
import math

import jax
import jax.numpy as jnp
from jax import lax
from jax.experimental import pallas as pl
from jax.experimental.pallas import tpu as pltpu
from jax.sharding import PartitionSpec as P

HD = 64
YS = 8
ZH = 4
ZL = 4
XS = 4
MESH = pl.DeviceIdType.MESH
F32 = jnp.float32
BF16 = jnp.bfloat16
SCALE = math.log2(math.e) / math.sqrt(HD)
VMEM_BYTES = 56 * 1024 * 1024


def push(src, dst, send_sem, recv_sem, device):
    return pltpu.make_async_remote_copy(
        src_ref=src,
        dst_ref=dst,
        send_sem=send_sem,
        recv_sem=recv_sem,
        device_id=device,
        device_id_type=MESH,
    )


def column_tiles(width, step):
    return [(start, min(step, width - start)) for start in range(0, width, step)]


def column_pieces(model, padded):
    cut = padded // 256 * 128
    tiles = column_tiles(cut, 768) + [(cut + a, b) for a, b in column_tiles(model - cut, 768)]
    return [(0, cut), (cut, padded - cut)], tiles


def barrier_with(devices):
    barrier = pltpu.get_barrier_semaphore()
    for device in devices:
        pl.semaphore_signal(barrier, inc=1, device_id=device, device_id_type=MESH)
    pl.semaphore_wait(barrier, len(devices))


def dot_t(a, b):
    return lax.dot_general(a, b, (((1,), (1,)), ((), ())), preferred_element_type=F32)


def layer_kernel(
    q_ref,
    kv_ref,
    wo_hbm,
    resid_ref,
    gain_ref,
    ids_ref,
    rw_ref,
    wgu_hbm,
    wd_hbm,
    attended_ref,
    mix_ref,
    kv_all,
    qt,
    vt,
    top,
    acc,
    attn,
    wo,
    part,
    sib,
    mine,
    landed,
    payload,
    rows_all,
    wgu,
    wd,
    made,
    from_sib,
    from_left,
    from_right,
    relays,
    total,
    ready,
    returned,
    w_sem,
    own_sem,
    a_send,
    a_recv,
    f_send,
    f_recv,
    b_send,
    b_recv,
    e_send,
    e_recv,
    c_send,
    c_recv,
    z_send,
    z_recv,
    x_send,
    x_recv,
    o_send,
    o_recv,
    s_send,
    s_recv,
    t_send,
    t_recv,
    p_send,
    p_recv,
    g_send,
    g_recv,
    k_send,
    k_recv,
    h_send,
    h_recv,
    r_send,
    r_recv,
):
    ctx = lax.axis_index("ctx")
    y, z = lax.div(ctx, ZH), lax.rem(ctx, ZH)
    exp = lax.axis_index("exp")
    zl, core = lax.div(exp, 2), lax.rem(exp, 2)
    x = lax.axis_index("dp")
    tokens, width = q_ref.shape
    heads = width // HD
    cols = tokens * heads
    rows, model = resid_ref.shape
    padded = payload.shape[1]
    hidden = wd.shape[1]
    pieces, tiles = column_pieces(model, padded)

    up = {"ctx": lax.rem(y + 1, YS) * ZH + z}
    down = {"ctx": lax.rem(y + YS - 1, YS) * ZH + z}
    z_peer = [{"ctx": y * ZH + lax.rem(z + d, ZH)} for d in range(ZH)]
    sibling = {"exp": zl * 2 + 1 - core}
    l_peer = [{"exp": lax.rem(zl + d, ZL) * 2 + core} for d in range(ZL)]
    left, right = lax.rem(x + XS - 1, XS), lax.rem(x + 1, XS)
    far = lax.rem(x + 2, XS)
    to_left, to_right = {"dp": left}, {"dp": right}

    w_copies = [
        pltpu.make_async_copy(wo_hbm, wo, w_sem.at[0]),
        pltpu.make_async_copy(wgu_hbm.at[0], wgu.at[0:model, 0:hidden], w_sem.at[1]),
        pltpu.make_async_copy(wgu_hbm.at[1], wgu.at[0:model, hidden : 2 * hidden], w_sem.at[2]),
        pltpu.make_async_copy(wd_hbm, wd, w_sem.at[3]),
    ]
    own_copy = pltpu.make_async_copy(kv_ref, kv_all.at[y, z], own_sem)
    own_copy.start()
    for copy in w_copies:
        copy.start()
    barrier_with([up, down, sibling, to_left, to_right] + z_peer[1:] + l_peer[1:])

    shift = [0, 1, 3, 2]
    started = []

    def settle():
        for finish in started:
            finish()
        started.clear()


    def gather_and_attend():
        column = [lax.rem(z + ZH - s, ZH) for s in shift]
        sends_up = y < YS - 1
        sends_down = y <= 2

        def block(group, j):
            return kv_all.at[group, column[j]]

        def forward(group, step, j):
            src = kv_ref if j == 0 and step == 0 else block(group, j)
            return push(src, block(group, j), f_send.at[step, j], f_recv.at[step, j], up)

        def backward(group, step, j):
            src = kv_ref if j == 0 and step == 0 else block(group, j)
            return push(src, block(group, j), b_send.at[step, j], b_recv.at[step, j], down)

        def z_push(j):
            return push(
                kv_ref, kv_all.at[y, z], a_send.at[j - 1], a_recv.at[j - 1], z_peer[shift[j]]
            )

        @pl.when(sends_up)
        def _():
            forward(y, 0, 0).start()

        @pl.when(sends_down)
        def _():
            backward(y, 0, 0).start()

        for j in (1, 2, 3):
            z_push(j).start()

        for pair in range(heads // 2):
            turned = q_ref[:, pair * 128 : pair * 128 + 128].astype(F32).T.astype(BF16)
            qt[0:HD, 2 * pair * tokens : (2 * pair + 1) * tokens] = turned[0:HD]
            qt[0:HD, (2 * pair + 1) * tokens : (2 * pair + 2) * tokens] = turned[HD:]
        qt[HD:, :] = jnp.zeros((128 - HD, cols), BF16)
        vt[HD:, :] = jnp.ones((vt.shape[0] - HD, vt.shape[1]), BF16)
        top[...] = jnp.full(top.shape, -1e30, F32)
        acc[...] = jnp.zeros(acc.shape, F32)
        wgu[model:, :] = jnp.zeros((padded - model, 2 * hidden), BF16)
        own_copy.wait()

        def attend(group, masked):
            for b in range(ZH):
                turned = kv_all[group, b].astype(F32).T
                vt[0:HD, b * tokens : (b + 1) * tokens] = turned[HD:].astype(BF16)
            keys = kv_all[group].reshape(ZH * tokens, 2 * HD)
            halves = [slice(0, cols // 2), slice(cols // 2, cols)]
            scores = [jnp.dot(keys, qt[:, lanes], preferred_element_type=F32) for lanes in halves]
            for lanes, seen in zip(halves, scores):
                if masked:
                    key_pos = lax.broadcasted_iota(jnp.int32, seen.shape, 0)
                    query_pos = lax.broadcasted_iota(jnp.int32, seen.shape, 1) % tokens + z * tokens
                    seen = jnp.where(key_pos <= query_pos, seen, -1e30)
                old = top[:, lanes]
                new = jnp.maximum(old, jnp.max(seen, axis=0, keepdims=True))
                probs = jnp.exp2((seen - new) * SCALE).astype(BF16)
                decay = jnp.exp2((old - new) * SCALE)
                top[:, lanes] = new
                acc[:, lanes] = acc[:, lanes] * decay + jnp.dot(
                    vt[...], probs, preferred_element_type=F32
                )

        for j in (1, 2, 3):
            z_push(j).wait_recv()

            @pl.when(sends_up)
            def _():
                forward(y, 0, j).start()

            @pl.when(sends_down)
            def _():
                backward(y, 0, j).start()

        attend(y, True)

        for step in (1, 2, 3, 4):
            group = y - step

            @pl.when(group >= 0)
            def _():
                for j in range(ZH):
                    forward(group, step - 1, j).wait_recv()
                    if step < 4:

                        @pl.when(sends_up)
                        def _():
                            forward(group, step, j).start()

                attend(group, False)

            if step < 4:
                wrapped = lax.rem(y + step, YS)

                @pl.when(wrapped <= 2)
                def _():
                    for j in range(ZH):
                        backward(wrapped, step - 1, j).wait_recv()
                        if step < 3:
                            backward(wrapped, step, j).start()

                    @pl.when(wrapped < y)
                    def _():
                        attend(wrapped, False)

        def finish():
            for j in (1, 2, 3):
                z_push(j).wait_send()
            for j in range(ZH):

                @pl.when(sends_up)
                def _():
                    forward(y, 0, j).wait_send()

                @pl.when(sends_down)
                def _():
                    backward(y, 0, j).wait_send()

                for step in (1, 2, 3):

                    @pl.when((y - step >= 0) & sends_up)
                    def _():
                        forward(y - step, step, j).wait_send()

                for step in (1, 2):

                    @pl.when(lax.rem(y + step, YS) <= 2)
                    def _():
                        backward(lax.rem(y + step, YS), step, j).wait_send()

        started.append(finish)

    def project():
        for pair in range(heads // 2):
            at = 2 * pair * tokens
            both = acc[:, at : at + 2 * tokens]
            ratio = both[0:HD] / both[HD : HD + 1]
            stacked = jnp.concatenate([ratio[:, :tokens], ratio[:, tokens:]], axis=0)
            attn[:, pair * 128 : pair * 128 + 128] = stacked.T.astype(BF16)
        w_copies[0].wait()

        def to_sibling(n):
            start, size = tiles[n]
            return push(
                part.at[1 - core, :, :, pl.ds(start, size)],
                sib.at[:, :, pl.ds(start, size)],
                e_send.at[n],
                e_recv.at[n],
                sibling,
            )

        for n, (start, size) in enumerate(tiles):
            out = dot_t(attn[...], wo[start : start + size, :]).astype(BF16)
            for d in range(2 * ZL):
                part[d % 2, d // 2, :, start : start + size] = out[d * rows : (d + 1) * rows]
            to_sibling(n).start()
        for n, (start, size) in enumerate(tiles):
            to_sibling(n).wait_recv()
            both = part[core, :, :, start : start + size].astype(F32) + sib[
                :, :, start : start + size
            ].astype(F32)
            mine[:, :, start : start + size] = both.astype(BF16)
            for piece in (0, 1):
                if start + size == min(sum(pieces[piece]), model):
                    for j in (1, 2, 3):
                        to_chip(j, piece).start()
        settle()
        started.append(lambda: [to_sibling(n).wait_send() for n in range(len(tiles))])
        started.append(
            lambda: [to_chip(j, piece).wait_send() for j in (1, 2, 3) for piece in (0, 1)]
        )

    def model_columns(piece):
        start, size = pieces[piece]
        return start, min(size, model - start)

    def to_chip(j, piece):
        lanes = pl.ds(*model_columns(piece))
        return push(
            mine.at[column[j], :, lanes],
            landed.at[zl, :, lanes],
            c_send.at[piece, j - 1],
            c_recv.at[piece, zl],
            {"exp": column[j] * 2 + core},
        )

    def finish_rows(piece, square):
        start, size = model_columns(piece)
        lanes = slice(start, start + size)
        projected = mine[zl, :, lanes].astype(F32)
        for j in (1, 2, 3):
            at = landed.at[column[j], :, pl.ds(start, size)]
            push(at, at, c_send.at[piece, 0], c_recv.at[piece, column[j]], sibling).wait_recv()
            projected = projected + landed[column[j], :, lanes].astype(F32)
        attended_ref[:, lanes] = projected.astype(BF16)
        state = resid_ref[:, lanes].astype(F32) + projected
        gain = gain_ref[lanes].reshape(1, size)
        payload[:, lanes] = (state * gain).astype(BF16)
        return square + jnp.sum(state * state, axis=-1, keepdims=True)

    def finish_tail(square):
        spare = padded - model
        place = lax.broadcasted_iota(jnp.int32, (rows, spare), 1)
        same = lax.broadcasted_iota(jnp.int32, (rows, rows), 0) == lax.broadcasted_iota(
            jnp.int32, (rows, rows), 1
        )
        weight = jnp.zeros((rows, spare), F32)
        for k in range(ids_ref.shape[0]):
            named = jnp.sum(
                jnp.where(same, ids_ref[k : k + 1, :].astype(F32), 0.0), axis=1, keepdims=True
            )
            share = jnp.sum(jnp.where(same, rw_ref[k : k + 1, :], 0.0), axis=1, keepdims=True)
            weight = weight + jnp.where(named == (place % 9).astype(F32), share, 0.0)
        inverse = lax.rsqrt(square / model + 1e-05)
        weight = jnp.where(place % 9 == 8, inverse, weight)
        high = weight.astype(BF16).astype(F32)
        middle = (weight - high).astype(BF16).astype(F32)
        low = weight - high - middle
        terms = jnp.where(place < 9, high, jnp.where(place < 18, middle, low))
        payload[:, model:] = jnp.where(place < 27, terms, 0.0).astype(BF16)

    side = lax.div(zl, 2)
    place_in = zl + side * (ZL - 1 - 2 * zl)
    column = [zl]
    for j in range(1, ZL):
        at = j - 1 + lax.div(j - 1 + ZL - place_in, ZL)
        column.append(at + side * (ZL - 1 - 2 * at))
    columns = [x, left, right, far]

    def slot(at, j, piece):
        return rows_all.at[at, core, column[j], :, pl.ds(*pieces[piece])]

    def expert(c):
        at = columns[c]
        inputs = rows_all[at].reshape(2 * ZL * rows, padded)
        both = jnp.dot(inputs, wgu[...], preferred_element_type=F32)
        tail = inputs[:, padded - 128 :].astype(F32)
        place = lax.broadcasted_iota(jnp.int32, tail.shape, 1) - (128 - (padded - model))

        def terms_of(n):
            chosen = (place == n) | (place == n + 9) | (place == n + 18)
            return jnp.sum(jnp.where(chosen, tail, 0.0), axis=1, keepdims=True)

        weight, inverse = terms_of(exp), terms_of(8)
        gate, upper = both[:, :hidden] * inverse, both[:, hidden:] * inverse
        active = (gate * jax.nn.sigmoid(1.702 * gate) * (upper + 1.0) * weight).astype(BF16)
        for start, size in column_tiles(model, 768):
            out = dot_t(active, wd[start : start + size, :]).astype(BF16)
            for d in range(2 * ZL):
                made[at, d // ZL, d % ZL, :, start : start + size] = out[d * rows : (d + 1) * rows]

    def p_push(c):
        return push(
            made.at[columns[c], 1 - core],
            from_sib.at[columns[c]],
            p_send.at[c],
            p_recv.at[c],
            sibling,
        )

    def pair_sum(c):
        p_push(c).wait_recv()
        at = columns[c]
        for b in range(ZL):
            made[at, core, b] = (made[at, core, b].astype(F32) + from_sib[at, b].astype(F32)).astype(
                BF16
            )

    def to_right_column(b):
        src = made.at[right, core, b]
        return push(src, from_left.at[b], g_send.at[b], g_recv.at[b], to_right)

    def to_left_column(b):
        src = made.at[left, core, b]
        return push(src, from_right.at[b], h_send.at[b], h_recv.at[b], to_left)

    def relay(b):
        src = made.at[far, core, b]
        dst = relays.at[b]
        return push(src, dst, k_send.at[b], k_recv.at[b], to_right if b < 2 else to_left)

    def gather_and_apply():
        def z_push(j, p):
            return push(
                source(0, p),
                slot(x, 0, p),
                z_send.at[p, j - 1],
                z_recv.at[p, zl],
                {"exp": column[j] * 2 + core},
            )

        def z_arrived(j, p):
            at = slot(x, j, p)
            push(at, at, z_send.at[p, j - 1], z_recv.at[p, column[j]], sibling).wait_recv()

        def source(j, p):
            return payload.at[:, pl.ds(*pieces[p])] if j == 0 else slot(x, j, p)

        def x_push(way, j, p):
            device = (to_right, to_left)[way]
            return push(
                source(j, p), slot(x, j, p), x_send.at[p, way, j], x_recv.at[p, way, j], device
            )

        def x_arrived(way, j, p):
            at = slot((left, right)[way], j, p)
            push(at, at, x_send.at[p, way, j], x_recv.at[p, way, j], to_right).wait_recv()

        def o_push(j, p):
            at = slot(left if j < 2 else right, j, p)
            return push(at, at, o_send.at[p, j], o_recv.at[p, j], to_right if j < 2 else to_left)

        def o_arrived(j, p):
            at = slot(far, j, p)
            push(at, at, o_send.at[p, j], o_recv.at[p, j], to_right).wait_recv()

        def s_push(c):
            at = rows_all.at[columns[c], core]
            return push(at, at, s_send.at[c], s_recv.at[c], sibling)

        def s_arrived(c):
            at = rows_all.at[columns[c], 1 - core]
            push(at, at, s_send.at[c], s_recv.at[c], sibling).wait_recv()

        def t_push(j):
            at = rows_all.at[far, core, column[j]]
            return push(at, at, t_send.at[j], t_recv.at[j], sibling)

        def t_arrived(j):
            at = rows_all.at[far, 1 - core, column[j]]
            push(at, at, t_send.at[j], t_recv.at[j], sibling).wait_recv()

        def start_rows(p):
            x_push(0, 0, p).start()
            x_push(1, 0, p).start()
            for j in (1, 2, 3):
                z_push(j, p).start()

        def z_forward(j, p):
            z_arrived(j, p)
            x_push(0, j, p).start()
            x_push(1, j, p).start()

        def x_forward(j, p):
            for way in (0, 1):
                x_arrived(way, j, p)
                if (j < 2) == (way == 0):
                    o_push(j, p).start()

        square = finish_rows(0, jnp.zeros((rows, 1), F32))
        start_rows(0)
        finish_tail(finish_rows(1, square))
        start_rows(1)
        own = pltpu.make_async_copy(payload, rows_all.at[x, core, zl], own_sem)
        own.start()
        x_forward(0, 0)
        z_forward(1, 0)
        x_forward(0, 1)
        z_forward(2, 0)
        x_forward(1, 0)
        z_forward(3, 0)
        x_forward(2, 0)
        z_forward(1, 1)
        x_forward(3, 0)
        z_forward(2, 1)
        x_forward(1, 1)
        z_forward(3, 1)
        own.wait()
        s_push(0).start()
        x_forward(2, 1)
        x_forward(3, 1)
        s_push(1).start()
        s_push(2).start()
        for copy in w_copies[1:]:
            copy.wait()
        s_arrived(1)
        expert(1)
        p_push(1).start()
        for j in range(ZL):
            o_arrived(j, 0)
            if j < 2:
                o_arrived(j, 1)
                t_push(j).start()
        s_arrived(2)
        expert(2)
        p_push(2).start()
        for j in (2, 3):
            o_arrived(j, 1)
            t_push(j).start()
        pair_sum(1)
        to_left_column(0).start()
        to_left_column(1).start()
        pair_sum(2)
        to_right_column(3).start()
        to_right_column(2).start()
        for j in range(ZL):
            t_arrived(j)
        expert(3)
        p_push(3).start()
        s_arrived(0)
        pair_sum(3)
        for b in (0, 1):
            relay(b).start()
            relay(3 - b).start()
        expert(0)
        p_push(0).start()

        def finish():
            for p in (0, 1):
                for j in (1, 2, 3):
                    z_push(j, p).wait_send()
                for j in range(ZL):
                    for way in (0, 1):
                        x_push(way, j, p).wait_send()
                    o_push(j, p).wait_send()
            for c in range(4):
                p_push(c).wait_send()
                t_push(c).wait_send()
                if c < 3:
                    s_push(c).wait_send()

        started.append(finish)

    def sum_columns():
        for b in (0, 3, 1, 2):
            relay(b).wait_recv()
            at = right if b < 2 else left
            made[at, core, b] = (made[at, core, b].astype(F32) + relays[b].astype(F32)).astype(BF16)
            if b < 2:
                to_right_column(b).start()
            else:
                to_left_column(b).start()
        pair_sum(0)

        def to_chip(b):
            return push(
                ready.at[b],
                returned.at[zl],
                r_send.at[b],
                r_recv.at[zl],
                {"exp": b * 2 + core},
            )

        for b in (0, 3, 1, 2):
            to_right_column(b).wait_recv()
            to_left_column(b).wait_recv()
            summed = (
                made[x, core, b].astype(F32) + from_left[b].astype(F32) + from_right[b].astype(F32)
            )
            total[b] = summed
            ready[b] = summed.astype(BF16)

            @pl.when(zl != b)
            def _():
                to_chip(b).start()

        settle()
        for b in range(ZL):
            to_right_column(b).wait_send()
            to_left_column(b).wait_send()
            relay(b).wait_send()
        mix = total[zl]
        for j in range(1, ZL):
            at = returned.at[column[j]]
            push(at, at, r_send.at[j], r_recv.at[column[j]], sibling).wait_recv()
            mix = mix + returned[column[j]].astype(F32)
        mix_ref[...] = mix.astype(BF16)

        def finish():
            for b in range(ZL):

                @pl.when(zl != b)
                def _():
                    to_chip(b).wait_send()

        started.append(finish)

    gather_and_attend()
    project()
    gather_and_apply()
    sum_columns()
    settle()


def layer(q, kv, wo, resid, gain, ids, rw, wgu, wd):
    tokens, width = q.shape
    cols = tokens * width // HD
    rows, model = resid.shape
    hidden = wd.shape[1]
    padded = -(-model // 128) * 128
    tiles = len(column_pieces(model, padded)[1])
    dma = pltpu.SemaphoreType.DMA
    vmem = pl.BlockSpec(memory_space=pltpu.VMEM)
    hbm = pl.BlockSpec(memory_space=pl.ANY)
    return pl.pallas_call(
        layer_kernel,
        out_shape=(
            jax.ShapeDtypeStruct((rows, model), BF16),
            jax.ShapeDtypeStruct((rows, model), BF16),
        ),
        in_specs=[vmem, vmem, hbm, vmem, vmem, vmem, vmem, hbm, hbm],
        out_specs=(vmem, vmem),
        scratch_shapes=[
            pltpu.VMEM((YS, ZH, tokens, 2 * HD), BF16),
            pltpu.VMEM((2 * HD, cols), BF16),
            pltpu.VMEM((HD + 16, ZH * tokens), BF16),
            pltpu.VMEM((1, cols), F32),
            pltpu.VMEM((HD + 16, cols), F32),
            pltpu.VMEM((tokens, width), BF16),
            pltpu.VMEM((model, width), BF16),
            pltpu.VMEM((2, ZL, rows, model), BF16),
            pltpu.VMEM((ZL, rows, model), BF16),
            pltpu.VMEM((ZL, rows, model), BF16),
            pltpu.VMEM((ZL, rows, model), BF16),
            pltpu.VMEM((rows, padded), BF16),
            pltpu.VMEM((XS, 2, ZL, rows, padded), BF16),
            pltpu.VMEM((padded, 2 * hidden), BF16),
            pltpu.VMEM((model, hidden), BF16),
            pltpu.VMEM((XS, 2, ZL, rows, model), BF16),
            pltpu.VMEM((XS, ZL, rows, model), BF16),
            pltpu.VMEM((ZL, rows, model), BF16),
            pltpu.VMEM((ZL, rows, model), BF16),
            pltpu.VMEM((ZL, rows, model), BF16),
            pltpu.VMEM((ZL, rows, model), F32),
            pltpu.VMEM((ZL, rows, model), BF16),
            pltpu.VMEM((ZL, rows, model), BF16),
            dma((4,)),
            dma,
        ]
        + [dma((ZH,))] * 2
        + [dma((4, ZH))] * 2
        + [dma((3, ZH))] * 2
        + [dma((tiles,))] * 2
        + [dma((2, ZL))] * 2
        + [dma((2, ZL))] * 2
        + [dma((2, 2, ZL))] * 2
        + [dma((2, ZL))] * 2
        + [dma((3,))] * 2
        + [dma((ZL,))] * 2
        + [dma((4,))] * 2
        + [dma((ZL,))] * 8,
        compiler_params=pltpu.CompilerParams(
            collective_id=0, has_side_effects=True, vmem_limit_bytes=VMEM_BYTES
        ),
    )(q, kv, wo, resid, gain, ids, rw, wgu, wd)


def shards(
    queries, key_values, out_weight, resid, norm_gain, expert_ids, route_weights, w_gate_up, w_down
):
    attended, mixture = layer(
        queries[0],
        key_values[0],
        out_weight.T,
        resid[0],
        norm_gain,
        expert_ids[0].T,
        route_weights[0].T,
        w_gate_up[0],
        w_down[0].T,
    )
    return attended[None], mixture[None]


def solution(mesh):
    return jax.shard_map(
        shards,
        mesh=mesh,
        in_specs=(
            P("dp", "ctx", "exp"),
            P("dp", "ctx", "exp"),
            P("exp", None),
            P("dp", ("ctx", "exp"), None),
            P(),
            P("dp", ("ctx", "exp"), None),
            P("dp", ("ctx", "exp"), None),
            P("exp", None, None, "dp"),
            P("exp", "dp", None),
        ),
        out_specs=(P("dp", ("ctx", "exp"), None), P("dp", ("ctx", "exp"), None)),
        check_vma=False,
    )
```
